32 devices in a mesh: groups: 2 (over x), tm: 16 (over z, y, core).
Axes of the slice: x: 2, y: 2, z: 4, core: 2. Of those that a mesh axis runs over, the one named last changes fastest.
Arguments:
- pixels: bfloat16 [128, 128, 1536], P(('groups', 'tm')), parts along dimension 0, as said below
- prior_kv: bfloat16 [2, 16, 128, 640], P(None, 'groups'), parts along dimension 1, may hold values from -6 to 6
- w_embed: bfloat16 [1536, 1280], replicated, may hold values from -0.15625 to 0.15625
- ln_gain: float32 [1280], replicated, may hold values from 0.1 to 1.9
- w_query: bfloat16 [1280, 640], replicated, as said below
- w_key: bfloat16 [1280, 640], replicated, as said below
- w_value: bfloat16 [1280, 640], replicated, may hold values from -0.15625 to 0.15625
- w_out: bfloat16 [640, 1280], replicated, may hold values from -0.25 to 0.25
Outputs:
- encoded: bfloat16 [128, 128, 1280], P(('groups', 'tm')), parts along dimension 0
The draws below stay inside these ranges and needn't reach their ends.
There are 2 independent parts, one for each index of `groups`. The reference program is written for one: setup_inputs(seed, part) draws one part's arguments, and reference() takes and returns one part's arrays. A program takes and returns all parts, laid end to end along the dimension named above; an argument that names none is the same for every part. Nothing has to cross between parts.
Inputs may be any that keep to these rules, and one draw needn't show every extreme that they name: `pixels`: standardized pixel values. `w_query`: query projection, entries of order 1280 ** -0.5. `w_key`: key projection.
All inputs are finite; a program needn't handle non-finite values.
Results may differ from the reference program's by a relative error of at most 0.007.
Values may be sent and summed in bfloat16 or wider, within the bound.
No kernel may reach another device: no remote copies, remote signals or barrier semaphores. Data moves between devices by JAX's collectives and lax.ppermute only.
A program may use at most 64 MiB of HBM per device.

```python
import math
import jax
import jax.numpy as jnp
from jax import lax

D = 1280
HEADS = 8
HEAD_DIM = 80
PIX = 1536
P_SIZE = 128
TUBELETS = 64
WINDOW = 8


def shared_matrix(key):
    return jax.random.truncated_normal(jax.random.fold_in(key, 11), -4.0, 4.0, (D, HEADS * HEAD_DIM), jnp.float32) * D ** (-0.5)


def draw_w_query(key, part):
    return shared_matrix(key).astype(jnp.bfloat16)


def draw_w_key(key, part):
    fresh = jax.random.truncated_normal(jax.random.fold_in(key, 31), -4.0, 4.0, (D, HEADS * HEAD_DIM), jnp.float32)
    return (fresh * D ** (-0.5)).astype(jnp.bfloat16)


def draw_pixels(key, part):
    shape = (TUBELETS, P_SIZE, PIX)
    return jax.random.truncated_normal(jax.random.fold_in(key, 53), -4.0, 4.0, shape, jnp.float32).astype(jnp.bfloat16)


def gaussian(stream_key, dims, scale, bound, kind=jnp.bfloat16):
    array = scale * jax.random.normal(stream_key, dims, jnp.float32)
    return jnp.clip(array, min=-bound, max=bound).astype(kind)


def setup_inputs(seed: int = 0, part: int = 0) -> dict:
    splits = jax.random.split(jax.random.key(seed), 9)
    part_keys = jax.random.split(jax.random.fold_in(splits[8], part), 9)
    return {
        "pixels": draw_pixels(jax.random.fold_in(jax.random.fold_in(splits[8], part), 71), part),
        "prior_kv": gaussian(part_keys[1], (2, WINDOW, P_SIZE, HEADS * HEAD_DIM), 1.0, 6.0),
        "w_embed": gaussian(splits[2], (PIX, D), PIX ** -0.5, 0.15625),
        "ln_gain": jnp.clip(1.0 + 0.18 * jax.random.normal(splits[3], (D,), jnp.float32), 0.1, 1.9),
        "w_query": draw_w_query(jax.random.fold_in(splits[8], 71), part),
        "w_key": draw_w_key(jax.random.fold_in(splits[8], 71), part),
        "w_value": gaussian(splits[6], (D, HEADS * HEAD_DIM), D ** -0.5, 0.15625),
        "w_out": gaussian(splits[7], (HEADS * HEAD_DIM, D), (HEADS * HEAD_DIM) ** -0.5, 0.25),
    }


def reference(pixels, prior_kv, w_embed, ln_gain, w_query, w_key, w_value, w_out):
    tub, pat, pix = pixels.shape
    flat = pixels.reshape(tub * pat, pix)
    embedded = jnp.dot(flat, w_embed, preferred_element_type=jnp.float32).astype(jnp.bfloat16)
    e_wide = embedded.astype(jnp.float32)
    center = e_wide - lax.optimization_barrier(jnp.mean(e_wide, axis=-1, keepdims=True))
    spread = lax.optimization_barrier(jnp.mean(center * center, axis=-1, keepdims=True))
    normed = (center * lax.rsqrt(spread + 1e-06) * ln_gain).astype(jnp.bfloat16)
    shape4 = (tub, pat, HEADS, HEAD_DIM)
    query = jnp.dot(normed, w_query, preferred_element_type=jnp.float32).astype(jnp.bfloat16).reshape(shape4)
    key = jnp.dot(normed, w_key, preferred_element_type=jnp.float32).astype(jnp.bfloat16).reshape(shape4)
    value = jnp.dot(normed, w_value, preferred_element_type=jnp.float32).astype(jnp.bfloat16).reshape(shape4)
    scale = 1.0 / math.sqrt(HEAD_DIM)
    prior_key = prior_kv[0].reshape(WINDOW, pat, HEADS, HEAD_DIM)
    prior_value = prior_kv[1].reshape(WINDOW, pat, HEADS, HEAD_DIM)
    key_pad = jnp.concatenate([prior_key, key], axis=0)
    value_pad = jnp.concatenate([prior_value, value], axis=0)
    query_wide = query.astype(jnp.float32)
    score_list = []
    for offset in range(WINDOW + 1):
        shifted = key_pad[WINDOW - offset:WINDOW - offset + tub].astype(jnp.float32)
        score_list.append(jnp.einsum('tphe,tphe->thp', query_wide, shifted) * scale)
    scores = jnp.stack(score_list, axis=0)
    top = lax.optimization_barrier(jnp.max(scores, axis=0, keepdims=True))
    expo = jnp.exp(scores - top)
    weights = (expo / lax.optimization_barrier(jnp.sum(expo, axis=0, keepdims=True))).astype(jnp.bfloat16)
    mixed = jnp.zeros((tub, pat, HEADS, HEAD_DIM), jnp.float32)
    for offset in range(WINDOW + 1):
        shifted = value_pad[WINDOW - offset:WINDOW - offset + tub].astype(jnp.float32)
        mixed = mixed + jnp.einsum('thp,tphe->tphe', weights[offset].astype(jnp.float32), shifted)
    mixed = mixed.astype(jnp.bfloat16).reshape(tub * pat, HEADS * HEAD_DIM)
    encoded = e_wide + jnp.dot(mixed, w_out, preferred_element_type=jnp.float32)
    return encoded.astype(jnp.bfloat16).reshape(tub, pat, D)
```

```python
import functools
import math

import jax
import jax.numpy as jnp
from jax import lax
from jax.experimental import pallas as pl
from jax.experimental.pallas import tpu as pltpu
from jax.sharding import PartitionSpec as P

HEADS = 8
HEAD_DIM = 80
BF = jnp.bfloat16
F32 = jnp.float32
ANY = pl.BlockSpec(memory_space=pl.ANY)
VMEM = pl.BlockSpec(memory_space=pltpu.VMEM)
SMEM = pl.BlockSpec(memory_space=pltpu.SMEM)
MIB = 1 << 20


def params(mib):
    return pltpu.CompilerParams(vmem_limit_bytes=mib * MIB)


COST = {"front": 37000, "second": 1, "ahead": 1300, "pack_key": 1, "pack_value": 1,
        "score": 1, "mix": 1, "finish": 1, "last": 1}


def call(kernel, name, mib, out_shape, in_specs, out_specs, scratch=(), aliases=None):
    return pl.pallas_call(
        kernel,
        out_shape=out_shape,
        in_specs=in_specs,
        out_specs=out_specs,
        scratch_shapes=list(scratch),
        input_output_aliases=aliases or {},
        compiler_params=params(mib),
        cost_estimate=pl.CostEstimate(flops=COST[name] * 10**6, bytes_accessed=1, transcendentals=0),
        name=name,
    )


def shape(dims, dtype=BF):
    return jax.ShapeDtypeStruct(dims, dtype)


def head_rows(h):
    return pl.ds(pl.multiple_of(h * HEAD_DIM, 16), HEAD_DIM)


def load_rows(source, target, sems):
    size = source.shape[0] // sems.shape[0]
    copies = []
    for i in range(sems.shape[0]):
        part = pl.ds(i * size, size)
        copies.append(pltpu.make_async_copy(source.at[part], target.at[part], sems.at[i]))
        copies[-1].start()
    return copies


def normed_rows(emb, part, gain):
    wide = emb[part, :].astype(F32)
    center = wide - jnp.mean(wide, axis=-1, keepdims=True)
    spread = jnp.mean(center * center, axis=-1, keepdims=True)
    return (center * lax.rsqrt(spread + 1e-06) * gain).astype(BF)


def project(nor, weight, turned, pat, blocks):
    size = nor.shape[0] // blocks
    for i in range(blocks):
        product = jnp.dot(
            nor[i * size:(i + 1) * size, :], weight[...], preferred_element_type=F32
        ).astype(BF)
        for u in range(size // pat):
            turned[i * (size // pat) + u] = product[u * pat:(u + 1) * pat, :].T


def store_parts(turned, parts, sem):
    copies = []
    for i, (target, start) in enumerate(parts):
        source = turned.at[pl.ds(start, target.shape[0])]
        copies.append(pltpu.make_async_copy(source, target, sem.at[i]))
        copies[-1].start()
    return copies


def front_kernel(pix_hbm, we_hbm, gain_ref, wk_hbm, e_hbm, n_hbm, ks_hbm, kl_hbm,
                 pix, we, wk, emb, nor, kt, sem, pix_sem, we_sem, out_sem):
    rows = pix.shape[0]
    tub, _, pat = kt.shape
    loads = load_rows(we_hbm, we, we_sem)
    pix_loads = load_rows(pix_hbm, pix, pix_sem)
    load_k = pltpu.make_async_copy(wk_hbm, wk, sem)
    load_k.start()
    for load in loads:
        load.wait()
    size = rows // len(pix_loads)
    for i, load in enumerate(pix_loads):
        load.wait()
        part = slice(i * size, (i + 1) * size)
        emb[part, :] = jnp.dot(pix[part, :], we[...], preferred_element_type=F32).astype(BF)
    gain = gain_ref[...].reshape(1, emb.shape[1])
    for i in range(len(pix_loads)):
        part = slice(i * size, (i + 1) * size)
        nor[part, :] = normed_rows(emb, part, gain)
    load_k.wait()
    project(nor, wk, kt, pat, len(pix_loads))
    stores = store_parts(kt, ((ks_hbm, 0), (kl_hbm, tub - 1)), out_sem)
    for i, (source, target) in enumerate(((nor, n_hbm), (emb, e_hbm))):
        stores.append(pltpu.make_async_copy(source, target, out_sem.at[2 + i]))
        stores[-1].start()
    for store in stores:
        store.wait()


def second_kernel(n_hbm, wv_hbm, wq_hbm, vo_hbm, ve_hbm, v_hbm, q_hbm,
                  nor, wv, wq, vt, qt, sem, out_sem):
    tub, _, pat = vt.shape
    loads = [
        pltpu.make_async_copy(source, target, sem.at[i])
        for i, (source, target) in enumerate(((n_hbm, nor), (wv_hbm, wv), (wq_hbm, wq)))
    ]
    for load in loads:
        load.start()
    loads[0].wait()
    loads[1].wait()
    project(nor, wv, vt, pat, 2)
    stores = store_parts(vt, ((vo_hbm, 0), (ve_hbm, 1), (v_hbm, 0)), out_sem)
    loads[2].wait()
    project(nor, wq, qt, pat, 2)
    stores.append(pltpu.make_async_copy(qt, q_hbm, out_sem.at[3]))
    stores[-1].start()
    for store in stores:
        store.wait()


def ahead_kernel(flag, pix_hbm, prior_hbm, we_hbm, gain_ref, wk_hbm, wv_hbm, out_hbm,
                 pix, we, wkv, emb, held, out, sem, we_sem, out_sem):
    _, tub, inner, pat = out.shape

    @pl.when(flag[0] == 1)
    def _():
        copies = [
            pltpu.make_async_copy(
                prior_hbm.at[i, pl.ds(flag[1] * tub, tub)], held.at[i], sem.at[i]
            )
            for i in range(2)
        ]
        for copy in copies:
            copy.start()
        for i in range(2):
            copies[i].wait()
            for t in range(tub):
                out[i, t] = held[i, t].T
        store = pltpu.make_async_copy(out, out_hbm, out_sem)
        store.start()
        store.wait()

    @pl.when(flag[0] == 0)
    def _():
        load_pix = pltpu.make_async_copy(pix_hbm, pix, sem.at[0])
        load_pix.start()
        loads = load_rows(we_hbm, we, we_sem)
        more = [
            pltpu.make_async_copy(source, wkv.at[i], sem.at[1 + i])
            for i, source in enumerate((wk_hbm, wv_hbm))
        ]
        for load in more:
            load.start()
        load_pix.wait()
        for load in loads:
            load.wait()
        emb[...] = jnp.dot(pix[...], we[...], preferred_element_type=F32).astype(BF)
        gain = gain_ref[...].reshape(1, emb.shape[1])
        nor = normed_rows(emb, slice(0, pat), gain)
        for i in range(2):
            more[i].wait()
            out[i, tub - 1] = jnp.dot(nor, wkv[i], preferred_element_type=F32).astype(BF).T
        store = pltpu.make_async_copy(
            out.at[:, pl.ds(tub - 1, 1)], out_hbm.at[:, pl.ds(tub - 1, 1)], out_sem
        )
        store.start()
        store.wait()


def pack_kernel(which, flag, own_ref, sent_ref, ahead_ref, *outs):
    tub = ahead_ref.shape[1]
    size = tub // len(outs)
    for t in range(tub):
        out = outs[t // size].at[t % size]

        @pl.when(flag[1] == 0)
        def _():
            out[...] = own_ref[t]

        @pl.when((flag[1] == 1) & (flag[0] == 1))
        def _():
            out[...] = ahead_ref[which, t]

        @pl.when((flag[1] == 1) & (flag[0] == 0))
        def _():
            out[...] = sent_ref[t] if t < tub - 1 else ahead_ref[which, t]


def take_far(flag, far, start, odd, even, kept):
    size = even.shape[0]
    where = slice(start, start + size)

    @pl.when(flag[0] == 1)
    def _():
        far[where] = kept[where]

    @pl.when((flag[0] == 0) & (flag[1] == 1))
    def _():
        far[where] = odd[where]

    @pl.when((flag[0] == 0) & (flag[1] == 0))
    def _():
        far[where] = even[...]


def score_kernel(flag, q_ref, sent_ref, ahead_ref, near0_ref, near1_ref, own_ref, w_ref, s_ref, far_ref):
    tub = q_ref.shape[0]
    reach = 2 * tub
    far_ref[tub - 1] = ahead_ref[0, tub - 1]

    @pl.when(flag[0] == 1)
    def _():
        far_ref[0:tub - 1] = ahead_ref[0, 0:tub - 1]

    @pl.when(flag[0] == 0)
    def _():
        far_ref[0:tub - 1] = sent_ref[...]

    keys = [ref.at[t] for ref in (far_ref, near0_ref, near1_ref, own_ref) for t in range(ref.shape[0])]

    def head(h, carry):
        part = head_rows(h)
        queries = [q_ref[t, part, :].astype(F32) for t in range(tub)]
        for j in range(3 * tub):
            key = keys[j][part, :].astype(F32)
            for t in range(max(0, j - reach), min(j, tub - 1) + 1):
                s_ref[t, j - t, pl.ds(h, 1), :] = jnp.sum(queries[t] * key, axis=0, keepdims=True)
        return carry

    lax.fori_loop(0, HEADS, head, 0)
    scale = 1.0 / math.sqrt(HEAD_DIM)
    for t in range(tub):
        scores = [s_ref[t, j] * scale for j in range(reach + 1)]
        top = functools.reduce(jnp.maximum, scores)
        expo = [jnp.exp(s - top) for s in scores]
        total = functools.reduce(jnp.add, expo)
        for j in range(reach + 1):
            w_ref[t, j] = (expo[j] / total).astype(BF).astype(F32)


def mix_kernel(pieces, w_ref, ahead_ref, *refs):
    near_refs = refs[:pieces]
    own_ref, e_ref, wo_ref, out_hbm, acc_ref, mix, out_vmem, sem = refs[pieces:]
    tub = own_ref.shape[0]
    reach = 2 * tub
    blocks = (ahead_ref.at[1], *near_refs, own_ref)
    values = [ref.at[t] for ref in blocks for t in range(ref.shape[0])]

    def head(h, carry):
        part = head_rows(h)
        sums = [None] * tub
        for j in range(tub - 1, 3 * tub):
            value = values[j][part, :].astype(F32)
            for t in range(max(0, j - reach), min(j, tub - 1) + 1):
                term = w_ref[t, j - t, pl.ds(h, 1), :] * value
                sums[t] = term if sums[t] is None else sums[t] + term
        for t in range(tub - 1):
            acc_ref[t, part, :] = sums[t]
        mix[part, :] = sums[tub - 1].astype(BF)
        return carry

    lax.fori_loop(0, HEADS, head, 0)
    finish_rows(mix[...], e_ref.at[tub - 1], wo_ref, out_vmem, out_hbm.at[tub - 1], sem).wait()


def finish_rows(mixed, e_ref, wo_ref, out_vmem, out_hbm, sem):
    product = jnp.dot(mixed.T, wo_ref[...], preferred_element_type=F32)
    out_vmem[...] = (e_ref[...].astype(F32) + product).astype(BF)
    store = pltpu.make_async_copy(out_vmem, out_hbm, sem)
    store.start()
    return store


def finish_kernel(start, stop, flag, w_ref, odd_ref, even_ref, ahead_ref, acc_ref, e_ref, wo_ref, _, out_hbm, *rest):
    if start:
        left_ref, far, mix, out_vmem, sem = rest
    else:
        far, mix, out_vmem, sem = rest
    take_far(flag, far, start, odd_ref, even_ref, ahead_ref.at[1])

    def head(h, carry):
        part = head_rows(h)
        values = {j: far[j, part, :].astype(F32) for j in range(start, stop)}
        for t in range(stop):
            total = acc_ref[t, part, :]
            for j in range(max(t, start), stop):
                total = total + w_ref[t, j - t, pl.ds(h, 1), :] * values[j]
            if t < start:
                left_ref[t, part, :] = total
            else:
                mix[t, part, :] = total.astype(BF)
        return carry

    lax.fori_loop(0, HEADS, head, 0)
    stores = [
        finish_rows(mix[t], e_ref.at[t], wo_ref, out_vmem.at[t], out_hbm.at[t], sem.at[t])
        for t in range(start, stop)
    ]
    for store in stores:
        store.wait()


def body(pixels, prior_kv, w_embed, ln_gain, w_query, w_key, w_value, w_out):
    tub, pat, pix = pixels.shape
    width, inner = w_query.shape
    rows, reach = tub * pat, 2 * tub
    count = lax.axis_size("tm")
    place = lax.axis_index("tm")
    flag = jnp.stack([(place < 2).astype(jnp.int32), place % 2])
    turned = (tub, inner, pat)
    most = (tub - 1, inner, pat)
    dma = pltpu.SemaphoreType.DMA

    def ring(value):
        return lax.ppermute(value, "tm", [(i, (i + 2) % count) for i in range(count)])

    def send_on(value, start):
        return lax.ppermute(value, "tm", [(i, i + 2) for i in range(start, count - 2, 2)])

    def swap(value):
        return lax.ppermute(value, "tm", [(i, i ^ 1) for i in range(count)])

    pix_ahead = ring(pixels[tub - 1])
    embedded, normed, key_most, key_rest = call(
        front_kernel, "front", 60,
        (shape((rows, width)), shape((rows, width)), shape(most), shape((1, inner, pat))),
        [ANY, ANY, VMEM, ANY], (ANY,) * 4,
        [
            pltpu.VMEM((rows, pix), BF), pltpu.VMEM((pix, width), BF), pltpu.VMEM((width, inner), BF),
            pltpu.VMEM((rows, width), BF), pltpu.VMEM((rows, width), BF), pltpu.VMEM(turned, BF),
            dma, dma((2,)), dma((4,)), dma((4,)),
        ],
    )(pixels.reshape(rows, pix), w_embed, ln_gain, w_key)
    key_sent = ring(key_most)
    value_most, value_mid, value, query = call(
        second_kernel, "second", 60,
        (shape(most), shape((tub - 2, inner, pat)), shape(turned), shape(turned)),
        [ANY, ANY, ANY], (ANY,) * 4,
        [
            pltpu.VMEM((rows, width), BF), pltpu.VMEM((width, inner), BF), pltpu.VMEM((width, inner), BF),
            pltpu.VMEM(turned, BF), pltpu.VMEM(turned, BF), dma((3,)), dma((4,)),
        ],
    )(normed, w_value, w_query)
    value_odd = send_on(value_most, 1)
    value_even = send_on(value_mid, 0)
    value_last = send_on(value[:1], 0)
    ahead = call(
        ahead_kernel, "ahead", 60,
        shape((2, *turned)),
        [SMEM, ANY, ANY, ANY, VMEM, ANY, ANY], ANY,
        [
            pltpu.VMEM((pat, pix), BF), pltpu.VMEM((pix, width), BF), pltpu.VMEM((2, width, inner), BF),
            pltpu.VMEM((pat, width), BF), pltpu.VMEM((2, tub, pat, inner), BF),
            pltpu.VMEM((2, *turned), BF), dma((3,)), dma((4,)), dma,
        ],
    )(flag, pix_ahead, prior_kv, w_embed, ln_gain, w_key, w_value)
    key = jnp.concatenate([key_most, key_rest], axis=0)

    def near(which, own, sent, name, pieces):
        parts = call(
            functools.partial(pack_kernel, which), name, 16,
            (shape((tub // pieces, inner, pat)),) * pieces,
            [SMEM, VMEM, VMEM, VMEM], (VMEM,) * pieces,
        )(flag, own, sent, ahead)
        return [swap(part) for part in parts]

    key_near = near(0, key, key_sent, "pack_key", 2)
    weights = call(
        score_kernel, "score", 16,
        shape((tub, reach + 1, HEADS, pat), F32),
        [SMEM] + [VMEM] * 6, VMEM,
        [pltpu.VMEM((tub, reach + 1, HEADS, pat), F32), pltpu.VMEM(turned, BF)],
    )(flag, query, key_sent, ahead, *key_near, key)
    value_odd, weights = lax.optimization_barrier((value_odd, weights))
    value_near = near(1, value, value_odd, "pack_value", tub)
    embedded = embedded.reshape(tub, pat, width)
    out, left = call(
        functools.partial(mix_kernel, tub), "mix", 24,
        (shape((tub, pat, width)), shape(most, F32)), [VMEM] * (5 + tub), (ANY, VMEM),
        [pltpu.VMEM((inner, pat), BF), pltpu.VMEM((pat, width), BF), dma],
    )(weights, ahead, *value_near, value, embedded, w_out)
    out, left = call(
        functools.partial(finish_kernel, 1, tub - 1), "finish", 24,
        (shape((tub, pat, width)), shape((1, inner, pat), F32)),
        [SMEM] + [VMEM] * 7 + [ANY], (ANY, VMEM),
        [
            pltpu.VMEM(most, BF), pltpu.VMEM(most, BF), pltpu.VMEM((tub - 1, pat, width), BF),
            dma((tub,)),
        ],
        {8: 0},
    )(flag, weights, value_odd, value_even, ahead, left, embedded, w_out, out)
    return call(
        functools.partial(finish_kernel, 0, 1), "last", 24,
        shape((tub, pat, width)),
        [SMEM] + [VMEM] * 7 + [ANY], ANY,
        [
            pltpu.VMEM((1, inner, pat), BF), pltpu.VMEM((1, inner, pat), BF),
            pltpu.VMEM((1, pat, width), BF), dma((1,)),
        ],
        {8: 0},
    )(flag, weights, value_odd, value_last, ahead, left, embedded, w_out, out)


def solution(mesh):
    placed = (
        P(("groups", "tm"), None, None),
        P(None, "groups", None, None),
        P(),
        P(),
        P(),
        P(),
        P(),
        P(),
    )
    return jax.shard_map(
        body, mesh=mesh, in_specs=placed, out_specs=P(("groups", "tm"), None, None), check_vma=False
    )
```

```python
import functools
import math

import jax
import jax.numpy as jnp
from jax import lax
from jax.experimental import pallas as pl
from jax.experimental.pallas import tpu as pltpu
from jax.sharding import PartitionSpec as P

HEADS = 8
HEAD_DIM = 80
BF = jnp.bfloat16
F32 = jnp.float32
ANY = pl.BlockSpec(memory_space=pl.ANY)
HBM = pl.BlockSpec(memory_space=pltpu.HBM)
VMEM = pl.BlockSpec(memory_space=pltpu.VMEM)
MIB = 1 << 20


def params(mib):
    return pltpu.CompilerParams(vmem_limit_bytes=mib * MIB)


COST = {"front": 37000, "second": 1, "ahead": 1300, "pack_key": 1, "pack_value": 1,
        "score": 1, "mix": 1, "finish": 1}
K_PIECES = 2
V_PIECES = 2


def call(kernel, name, mib, out_shape, in_specs, out_specs, scratch=(), aliases=None):
    return pl.pallas_call(
        kernel,
        out_shape=out_shape,
        in_specs=in_specs,
        out_specs=out_specs,
        scratch_shapes=list(scratch),
        input_output_aliases=aliases or {},
        compiler_params=params(mib),
        cost_estimate=pl.CostEstimate(flops=COST[name] * 10**6, bytes_accessed=1, transcendentals=0),
        name=name,
    )


def shape(dims, dtype=BF):
    return jax.ShapeDtypeStruct(dims, dtype)


def head_rows(h):
    return pl.ds(pl.multiple_of(h * HEAD_DIM, 16), HEAD_DIM)


def normed_rows(emb, part, gain):
    wide = emb[part, :].astype(F32)
    center = wide - jnp.mean(wide, axis=-1, keepdims=True)
    spread = jnp.mean(center * center, axis=-1, keepdims=True)
    return (center * lax.rsqrt(spread + 1e-06) * gain).astype(BF)


def copy_in(pairs, sems):
    copies = [
        pltpu.make_async_copy(source, target, sems.at[i]) for i, (source, target) in enumerate(pairs)
    ]
    for copy in copies:
        copy.start()
    return copies


def position():
    place = lax.axis_index("tm")
    return place < 2, lax.rem(place, 2) == 1


def front_kernel(pix_hbm, we_hbm, gain_hbm, wk_hbm, wv_hbm, wq_hbm, wo_hbm,
                 emb, nor, key_most, key_rest, we, gain_ref, wk, wv, wq, wo, pix, we_sem, sem):
    rows, width = emb.shape
    tub = key_most.shape[0] + 1
    pat = rows // tub
    size, cut = rows // 2, width // 5 * 2
    parts = [slice(i * size, (i + 1) * size) for i in range(2)]
    halves = [slice(0, cut), slice(cut, width)]
    loads = copy_in(
        [
            (pix_hbm.at[pl.ds(0, size)], pix.at[pl.ds(0, size)]),
            (we_hbm.at[:, pl.ds(0, cut)], we.at[:, pl.ds(0, cut)]),
            (pix_hbm.at[pl.ds(size, size)], pix.at[pl.ds(size, size)]),
            (we_hbm.at[:, pl.ds(cut, width - cut)], we.at[:, pl.ds(cut, width - cut)]),
        ],
        we_sem,
    )
    more = copy_in(
        [(gain_hbm, gain_ref), (wk_hbm, wk), (wv_hbm, wv), (wq_hbm, wq), (wo_hbm, wo)], sem
    )
    for j, half in enumerate(halves):
        for i, part in enumerate(parts):
            if j == 0:
                loads[2 * i].wait()
            if i == 0:
                loads[1 + 2 * j].wait()
            emb[part, half] = jnp.dot(
                pix[part, :], we[:, half], preferred_element_type=F32
            ).astype(BF)
    more[0].wait()
    gain = gain_ref[...].reshape(1, width)
    for t in range(tub):
        part = slice(t * pat, (t + 1) * pat)
        nor[part, :] = normed_rows(emb, part, gain)
    more[1].wait()
    for i, part in enumerate(parts):
        product = jnp.dot(nor[part, :], wk[...], preferred_element_type=F32).astype(BF)
        for u in range(size // pat):
            t = i * (size // pat) + u
            turned = product[u * pat:(u + 1) * pat, :].T
            if t < tub - 1:
                key_most[t] = turned
            else:
                key_rest[0] = turned
    for load in more[2:]:
        load.wait()


def tubelets(refs):
    return [ref.at[t] for ref in refs for t in range(ref.shape[0])]


def second_kernel(nor, wv, wq, value_most, query, *values):
    tub, _, pat = query.shape
    size = nor.shape[0] // 2
    for weight, target in ((wv, tubelets(values)), (wq, tubelets([query]))):
        for i in range(2):
            product = jnp.dot(
                nor[i * size:(i + 1) * size, :], weight[...], preferred_element_type=F32
            ).astype(BF)
            for u in range(size // pat):
                t = i * (size // pat) + u
                turned = product[u * pat:(u + 1) * pat, :].T
                target[t][...] = turned
                if weight is wv and t < tub - 1:
                    value_most[t] = turned


def ahead_kernel(pix, prior_hbm, we, gain_ref, wk, wv, out, value_last, emb, held, sem):
    tub = out.shape[1] // 2
    pat = out.shape[3]
    first, second = position()

    @pl.when(first)
    def _():
        copies = copy_in([(prior_hbm.at[i], held.at[i]) for i in range(2)], sem)
        for i in range(2):
            copies[i].wait()
            for t in range(2 * tub):
                there = (t + second.astype(jnp.int32) * tub) % (2 * tub)
                out[i, t] = held[i, there].T

    @pl.when(jnp.logical_not(first))
    def _():
        emb[...] = jnp.dot(pix[...], we[...], preferred_element_type=F32).astype(BF)
        gain = gain_ref[...].reshape(1, emb.shape[1])
        nor = normed_rows(emb, slice(0, pat), gain)
        for i, weight in enumerate((wk, wv)):
            turned = jnp.dot(nor, weight[...], preferred_element_type=F32).astype(BF).T
            out[i, tub - 1] = turned
            if i == 1:
                value_last[0] = turned


def pack_key_kernel(most_ref, rest_ref, sent_ref, ahead_ref, *outs):
    tub = most_ref.shape[0] + 1
    size = tub // len(outs)
    _, second = position()
    for t in range(tub):
        out = outs[t // size].at[t % size]

        @pl.when(jnp.logical_not(second))
        def _():
            out[...] = most_ref[t] if t < tub - 1 else rest_ref[0]

        @pl.when(second)
        def _():
            out[...] = sent_ref[t] if t < tub - 1 else ahead_ref[0, t]


def pack_value_kernel(most_ref, *refs):
    *swapped_refs, out_ref = refs
    tub, half, _ = out_ref.shape
    _, second = position()

    @pl.when(jnp.logical_not(second))
    def _():
        for t, ref in enumerate(tubelets(swapped_refs)[:tub]):
            out_ref[t] = ref[0:half, :]

    @pl.when(second)
    def _():
        out_ref[...] = most_ref[:, half:, :]


def score_kernel(pieces, q_ref, sent_ref, ahead_ref, *refs):
    near_refs = refs[:pieces]
    most_ref, rest_ref, w_ref, s_ref, far_ref, near_ref = refs[pieces:]
    tub = q_ref.shape[0]
    reach = 2 * tub
    first, second = position()
    far_ref[tub - 1] = ahead_ref[0, tub - 1]

    @pl.when(first)
    def _():
        far_ref[0:tub - 1] = ahead_ref[0, 0:tub - 1]

    @pl.when(jnp.logical_not(first))
    def _():
        far_ref[0:tub - 1] = sent_ref[...]

    @pl.when(first & jnp.logical_not(second))
    def _():
        near_ref[...] = ahead_ref[0, tub:]

    @pl.when(jnp.logical_not(first) | second)
    def _():
        for t in range(tub):
            near_ref[t] = tubelets(near_refs)[t][...]

    keys = tubelets((far_ref, near_ref, most_ref, rest_ref))

    def head(h, carry):
        part = head_rows(h)
        queries = [q_ref[t, part, :].astype(F32) for t in range(tub)]
        for j in range(3 * tub):
            key = keys[j][part, :].astype(F32)
            for t in range(max(0, j - reach), min(j, tub - 1) + 1):
                s_ref[t, j - t, pl.ds(h, 1), :] = jnp.sum(queries[t] * key, axis=0, keepdims=True)
        return carry

    lax.fori_loop(0, HEADS, head, 0)
    scale = 1.0 / math.sqrt(HEAD_DIM)
    for t in range(tub):
        scores = [s_ref[t, j] * scale for j in range(reach + 1)]
        top = functools.reduce(jnp.maximum, scores)
        expo = [jnp.exp(s - top) for s in scores]
        total = functools.reduce(jnp.add, expo)
        for j in range(reach + 1):
            w_ref[t, j] = (expo[j] / total).astype(BF).astype(F32)


def mix_kernel(pieces, w_ref, ahead_ref, held_ref, other_ref, last_ref, e_ref, wo_ref, *refs):
    swapped, own = tubelets(refs[:pieces]), tubelets(refs[pieces:2 * pieces])
    out_hbm, acc_ref, odd_ref, near_ref, mix, out_vmem, sem = refs[2 * pieces:]
    tub = len(own)
    reach = 2 * tub
    half = held_ref.shape[1]
    first, second = position()

    @pl.when(second)
    def _():
        odd_ref[:, 0:half, :] = other_ref[...]
        odd_ref[:, half:, :] = held_ref[...]
        for t in range(tub):
            near_ref[t] = swapped[t][...]

    @pl.when(jnp.logical_not(second) & jnp.logical_not(first))
    def _():
        near_ref[0:tub - 1, 0:half, :] = held_ref[...]
        near_ref[0:tub - 1, half:, :] = other_ref[...]
        near_ref[tub - 1] = last_ref[0]

    @pl.when(jnp.logical_not(second) & first)
    def _():
        near_ref[...] = ahead_ref[1, tub:]

    values = [ahead_ref.at[1, tub - 1], *tubelets([near_ref]), *own]

    def head(h, carry):
        part = head_rows(h)
        sums = [None] * tub
        for j in range(tub - 1, 3 * tub):
            value = values[j - tub + 1][part, :].astype(F32)
            for t in range(max(0, j - reach), min(j, tub - 1) + 1):
                term = w_ref[t, j - t, pl.ds(h, 1), :] * value
                sums[t] = term if sums[t] is None else sums[t] + term
        for t in range(tub - 1):
            acc_ref[t, part, :] = sums[t]
        mix[part, :] = sums[tub - 1].astype(BF)
        return carry

    lax.fori_loop(0, HEADS, head, 0)
    finish_rows(mix[...], e_ref.at[tub - 1], wo_ref, out_vmem, out_hbm.at[tub - 1], sem).wait()


def finish_rows(mixed, e_ref, wo_ref, out_vmem, out_hbm, sem):
    product = jnp.dot(mixed.T, wo_ref[...], preferred_element_type=F32)
    out_vmem[...] = (e_ref[...].astype(F32) + product).astype(BF)
    store = pltpu.make_async_copy(out_vmem, out_hbm, sem)
    store.start()
    return store


def finish_kernel(w_ref, odd_ref, even_ref, ahead_ref, acc_ref, e_ref, wo_ref, _, out_hbm, far, mix, out_vmem, sem):
    count = far.shape[0]
    first, second = position()

    @pl.when(first)
    def _():
        far[...] = ahead_ref[1, 0:count]

    @pl.when(jnp.logical_not(first) & second)
    def _():
        far[...] = odd_ref[...]

    @pl.when(jnp.logical_not(first) & jnp.logical_not(second))
    def _():
        far[...] = even_ref[...]

    def head(h, carry):
        part = head_rows(h)
        values = [far[j, part, :].astype(F32) for j in range(count)]
        for t in range(count):
            total = acc_ref[t, part, :]
            for j in range(t, count):
                total = total + w_ref[t, j - t, pl.ds(h, 1), :] * values[j]
            mix[t, part, :] = total.astype(BF)
        return carry

    lax.fori_loop(0, HEADS, head, 0)
    stores = [
        finish_rows(mix[t], e_ref.at[t], wo_ref, out_vmem.at[t], out_hbm.at[t], sem.at[t])
        for t in range(count)
    ]
    for store in stores:
        store.wait()


def body(pixels, prior_kv, w_embed, ln_gain, w_query, w_key, w_value, w_out):
    tub, pat, pix = pixels.shape
    width, inner = w_query.shape
    rows, reach = tub * pat, 2 * tub
    count = lax.axis_size("tm")
    turned = (tub, inner, pat)
    most, rest = (tub - 1, inner, pat), (1, inner, pat)
    dma = pltpu.SemaphoreType.DMA

    def in_hbm(value):
        return pltpu.with_memory_space_constraint(value, pltpu.HBM)

    def ring(value):
        return lax.ppermute(value, "tm", [(i, (i + 2) % count) for i in range(count)])

    def shift(value, start=0, step=1):
        return lax.ppermute(value, "tm", [(i, i + 2) for i in range(start, count - 2, step)])

    def swap(value):
        return lax.ppermute(value, "tm", [(i, i ^ 1) for i in range(count)])

    pix_ahead = ring(pixels[tub - 1])
    embedded, normed, key_most, key_rest, w_embed, ln_gain, w_key, w_value, w_query, w_out = call(
        front_kernel, "front", 24,
        (
            shape((rows, width)), shape((rows, width)), shape(most), shape(rest),
            shape(w_embed.shape), shape(ln_gain.shape, F32), shape(w_key.shape),
            shape(w_value.shape), shape(w_query.shape), shape(w_out.shape),
        ),
        [HBM] * 7, (VMEM,) * 10,
        [pltpu.VMEM((rows, pix), BF), dma((4,)), dma((5,))],
    )(
        in_hbm(pixels.reshape(rows, pix)), in_hbm(w_embed), in_hbm(ln_gain),
        in_hbm(w_key), in_hbm(w_value), in_hbm(w_query), in_hbm(w_out),
    )
    key_sent = ring(key_most)
    value_most, query, *value = call(
        second_kernel, "second", 16,
        (shape(most), shape(turned), *[shape((tub // V_PIECES, inner, pat))] * V_PIECES),
        [VMEM] * 3, (VMEM,) * (2 + V_PIECES),
    )(normed, w_value, w_query)
    value_swapped = [swap(part) for part in value]
    value_half = shift(
        call(
            pack_value_kernel, "pack_value", 16,
            shape((tub - 1, inner // 2, pat)), [VMEM] * (1 + V_PIECES), VMEM,
        )(value_most, *value_swapped)
    )
    value_even = shift(value_most, 0, 2)
    ahead, value_last = call(
        ahead_kernel, "ahead", 24,
        (shape((2, reach, inner, pat)), shape(rest)),
        [VMEM, HBM, VMEM, VMEM, VMEM, VMEM], (VMEM,) * 2,
        [pltpu.VMEM((pat, width), BF), pltpu.VMEM((2, reach, pat, inner), BF), dma((2,))],
    )(pix_ahead, in_hbm(prior_kv), w_embed, ln_gain, w_key, w_value)
    key_near = [
        swap(part)
        for part in call(
            pack_key_kernel, "pack_key", 16,
            (shape((tub // K_PIECES, inner, pat)),) * K_PIECES,
            [VMEM] * 4, (VMEM,) * K_PIECES,
        )(key_most, key_rest, key_sent, ahead)
    ]
    value_last = swap(value_last)
    weights = call(
        functools.partial(score_kernel, K_PIECES), "score", 16,
        shape((tub, reach + 1, HEADS, pat), F32),
        [VMEM] * (5 + K_PIECES), VMEM,
        [
            pltpu.VMEM((tub, reach + 1, HEADS, pat), F32), pltpu.VMEM(turned, BF),
            pltpu.VMEM(turned, BF),
        ],
    )(query, key_sent, ahead, *key_near, key_most, key_rest)
    value_other = swap(value_half)
    embedded = embedded.reshape(tub, pat, width)
    out, left, odd = call(
        functools.partial(mix_kernel, V_PIECES), "mix", 24,
        (shape((tub, pat, width)), shape(most, F32), shape(most)),
        [VMEM] * (7 + 2 * V_PIECES), (ANY, VMEM, VMEM),
        [pltpu.VMEM(turned, BF), pltpu.VMEM((inner, pat), BF), pltpu.VMEM((pat, width), BF), dma],
    )(weights, ahead, value_half, value_other, value_last, embedded, w_out, *value_swapped, *value)
    return call(
        finish_kernel, "finish", 24,
        shape((tub, pat, width)),
        [VMEM] * 7 + [ANY], ANY,
        [
            pltpu.VMEM(most, BF), pltpu.VMEM(most, BF), pltpu.VMEM((tub - 1, pat, width), BF),
            dma((tub,)),
        ],
        {7: 0},
    )(weights, odd, value_even, ahead, left, embedded, w_out, out)


def solution(mesh):
    placed = (
        P(("groups", "tm"), None, None),
        P(None, "groups", None, None),
        P(),
        P(),
        P(),
        P(),
        P(),
        P(),
    )
    return jax.shard_map(
        body, mesh=mesh, in_specs=placed, out_specs=P(("groups", "tm"), None, None), check_vma=False
    )
```

```python
import functools
import math

import jax
import jax.numpy as jnp
from jax import lax
from jax.experimental import pallas as pl
from jax.experimental.pallas import tpu as pltpu
from jax.sharding import PartitionSpec as P

HEADS = 8
HEAD_DIM = 80
BF = jnp.bfloat16
F32 = jnp.float32
ANY = pl.BlockSpec(memory_space=pl.ANY)
HBM = pl.BlockSpec(memory_space=pltpu.HBM)
VMEM = pl.BlockSpec(memory_space=pltpu.VMEM)
MIB = 1 << 20


def params(mib):
    return pltpu.CompilerParams(vmem_limit_bytes=mib * MIB)


COST = {"front": 37000, "second": 1, "ahead": 1300, "pack_key": 1, "pack_value": 1,
        "score": 1, "mix": 1, "finish": 1}
K_PIECES = 2
V_PIECES = 2


def call(kernel, name, mib, out_shape, in_specs, out_specs, scratch=(), aliases=None):
    return pl.pallas_call(
        kernel,
        out_shape=out_shape,
        in_specs=in_specs,
        out_specs=out_specs,
        scratch_shapes=list(scratch),
        input_output_aliases=aliases or {},
        compiler_params=params(mib),
        cost_estimate=pl.CostEstimate(flops=COST[name] * 10**6, bytes_accessed=1, transcendentals=0),
        name=name,
    )


def shape(dims, dtype=BF):
    return jax.ShapeDtypeStruct(dims, dtype)


def head_rows(h):
    return pl.ds(pl.multiple_of(h * HEAD_DIM, 16), HEAD_DIM)


def normed_rows(emb, part, gain):
    wide = emb[part, :].astype(F32)
    center = wide - jnp.mean(wide, axis=-1, keepdims=True)
    spread = jnp.mean(center * center, axis=-1, keepdims=True)
    return (center * lax.rsqrt(spread + 1e-06) * gain).astype(BF)


def copy_in(pairs, sems):
    copies = [
        pltpu.make_async_copy(source, target, sems.at[i]) for i, (source, target) in enumerate(pairs)
    ]
    for copy in copies:
        copy.start()
    return copies


def position():
    place = lax.axis_index("tm")
    return place < 2, lax.rem(place, 2) == 1


def front_kernel(pix_hbm, we_hbm, gain_hbm, wk_hbm, wv_hbm, wq_hbm, wo_hbm,
                 emb, nor, key_most, key_rest, we, gain_ref, wk, wv, wq, wo, pix, we_sem, sem, late_sem):
    rows, width = emb.shape
    tub = key_most.shape[0] + 1
    pat = rows // tub
    size, cut = rows // 2, width // 5 * 2
    parts = [slice(i * size, (i + 1) * size) for i in range(2)]
    halves = [slice(0, cut), slice(cut, width)]
    loads = copy_in(
        [
            (pix_hbm.at[pl.ds(0, size)], pix.at[pl.ds(0, size)]),
            (we_hbm.at[:, pl.ds(0, cut)], we.at[:, pl.ds(0, cut)]),
            (pix_hbm.at[pl.ds(size, size)], pix.at[pl.ds(size, size)]),
            (we_hbm.at[:, pl.ds(cut, width - cut)], we.at[:, pl.ds(cut, width - cut)]),
        ],
        we_sem,
    )
    more = copy_in([(gain_hbm, gain_ref), (wk_hbm, wk)], sem)
    for j, half in enumerate(halves):
        for i, part in enumerate(parts):
            if j == 0:
                loads[2 * i].wait()
            if i == 0:
                loads[1 + 2 * j].wait()
            if i == j == 1:
                later = copy_in([(wv_hbm, wv), (wq_hbm, wq), (wo_hbm, wo)], late_sem)
            emb[part, half] = jnp.dot(
                pix[part, :], we[:, half], preferred_element_type=F32
            ).astype(BF)
    more[0].wait()
    gain = gain_ref[...].reshape(1, width)
    for t in range(tub):
        part = slice(t * pat, (t + 1) * pat)
        nor[part, :] = normed_rows(emb, part, gain)
    more[1].wait()
    for i, part in enumerate(parts):
        product = jnp.dot(nor[part, :], wk[...], preferred_element_type=F32).astype(BF)
        for u in range(size // pat):
            t = i * (size // pat) + u
            turned = product[u * pat:(u + 1) * pat, :].T
            if t < tub - 1:
                key_most[t] = turned
            else:
                key_rest[0] = turned
    for load in later:
        load.wait()


def tubelets(refs):
    return [ref.at[t] for ref in refs for t in range(ref.shape[0])]


def second_kernel(nor, wv, wq, value_most, query, *values):
    tub, _, pat = query.shape
    size = nor.shape[0] // 2
    for weight, target in ((wv, tubelets(values)), (wq, tubelets([query]))):
        for i in range(2):
            product = jnp.dot(
                nor[i * size:(i + 1) * size, :], weight[...], preferred_element_type=F32
            ).astype(BF)
            for u in range(size // pat):
                t = i * (size // pat) + u
                turned = product[u * pat:(u + 1) * pat, :].T
                target[t][...] = turned
                if weight is wv and t < tub - 1:
                    value_most[t] = turned


def ahead_kernel(pix, prior_hbm, we, gain_ref, wk, wv, out, value_last, emb, held, sem):
    tub = out.shape[1] // 2
    pat = out.shape[3]
    first, second = position()

    @pl.when(first)
    def _():
        copies = copy_in([(prior_hbm.at[i], held.at[i]) for i in range(2)], sem)
        for i in range(2):
            copies[i].wait()
            for t in range(2 * tub):
                there = (t + second.astype(jnp.int32) * tub) % (2 * tub)
                out[i, t] = held[i, there].T

    @pl.when(jnp.logical_not(first))
    def _():
        emb[...] = jnp.dot(pix[...], we[...], preferred_element_type=F32).astype(BF)
        gain = gain_ref[...].reshape(1, emb.shape[1])
        nor = normed_rows(emb, slice(0, pat), gain)
        for i, weight in enumerate((wk, wv)):
            turned = jnp.dot(nor, weight[...], preferred_element_type=F32).astype(BF).T
            out[i, tub - 1] = turned
            if i == 1:
                value_last[0] = turned


def pack_key_kernel(most_ref, rest_ref, sent_ref, ahead_ref, *outs):
    tub = most_ref.shape[0] + 1
    size = tub // len(outs)
    _, second = position()
    for t in range(tub):
        out = outs[t // size].at[t % size]

        @pl.when(jnp.logical_not(second))
        def _():
            out[...] = most_ref[t] if t < tub - 1 else rest_ref[0]

        @pl.when(second)
        def _():
            out[...] = sent_ref[t] if t < tub - 1 else ahead_ref[0, t]


def pack_value_kernel(most_ref, *refs):
    *swapped_refs, out_ref = refs
    tub, half, _ = out_ref.shape
    _, second = position()

    @pl.when(jnp.logical_not(second))
    def _():
        for t, ref in enumerate(tubelets(swapped_refs)[:tub]):
            out_ref[t] = ref[0:half, :]

    @pl.when(second)
    def _():
        out_ref[...] = most_ref[:, half:, :]


def score_kernel(pieces, q_ref, sent_ref, ahead_ref, *refs):
    near_refs = refs[:pieces]
    most_ref, rest_ref, w_ref, s_ref, far_ref, near_ref = refs[pieces:]
    tub = q_ref.shape[0]
    reach = 2 * tub
    first, second = position()
    far_ref[tub - 1] = ahead_ref[0, tub - 1]

    @pl.when(first)
    def _():
        far_ref[0:tub - 1] = ahead_ref[0, 0:tub - 1]

    @pl.when(jnp.logical_not(first))
    def _():
        far_ref[0:tub - 1] = sent_ref[...]

    @pl.when(first & jnp.logical_not(second))
    def _():
        near_ref[...] = ahead_ref[0, tub:]

    @pl.when(jnp.logical_not(first) | second)
    def _():
        for t in range(tub):
            near_ref[t] = tubelets(near_refs)[t][...]

    keys = tubelets((far_ref, near_ref, most_ref, rest_ref))

    def head(h, carry):
        part = head_rows(h)
        queries = [q_ref[t, part, :].astype(F32) for t in range(tub)]
        for j in range(3 * tub):
            key = keys[j][part, :].astype(F32)
            for t in range(max(0, j - reach), min(j, tub - 1) + 1):
                s_ref[t, j - t, pl.ds(h, 1), :] = jnp.sum(queries[t] * key, axis=0, keepdims=True)
        return carry

    lax.fori_loop(0, HEADS, head, 0)
    scale = 1.0 / math.sqrt(HEAD_DIM)
    for t in range(tub):
        scores = [s_ref[t, j] * scale for j in range(reach + 1)]
        top = functools.reduce(jnp.maximum, scores)
        expo = [jnp.exp(s - top) for s in scores]
        total = functools.reduce(jnp.add, expo)
        for j in range(reach + 1):
            w_ref[t, j] = (expo[j] / total).astype(BF).astype(F32)


def mix_kernel(pieces, w_ref, ahead_ref, held_ref, other_ref, last_ref, e_ref, wo_ref, *refs):
    swapped, own = tubelets(refs[:pieces]), tubelets(refs[pieces:2 * pieces])
    out_hbm, acc_ref, odd_ref, near_ref, mix, out_vmem, sem = refs[2 * pieces:]
    tub = len(own)
    reach = 2 * tub
    half = held_ref.shape[1]
    first, second = position()

    @pl.when(second)
    def _():
        odd_ref[:, 0:half, :] = other_ref[...]
        odd_ref[:, half:, :] = held_ref[...]
        for t in range(tub):
            near_ref[t] = swapped[t][...]

    @pl.when(jnp.logical_not(second) & jnp.logical_not(first))
    def _():
        near_ref[0:tub - 1, 0:half, :] = held_ref[...]
        near_ref[0:tub - 1, half:, :] = other_ref[...]
        near_ref[tub - 1] = last_ref[0]

    @pl.when(jnp.logical_not(second) & first)
    def _():
        near_ref[...] = ahead_ref[1, tub:]

    values = [ahead_ref.at[1, tub - 1], *tubelets([near_ref]), *own]

    def head(h, carry):
        part = head_rows(h)
        sums = [None] * tub
        for j in range(tub - 1, 3 * tub):
            value = values[j - tub + 1][part, :].astype(F32)
            for t in range(max(0, j - reach), min(j, tub - 1) + 1):
                term = w_ref[t, j - t, pl.ds(h, 1), :] * value
                sums[t] = term if sums[t] is None else sums[t] + term
        for t in range(tub - 1):
            acc_ref[t, part, :] = sums[t]
        mix[part, :] = sums[tub - 1].astype(BF)
        return carry

    lax.fori_loop(0, HEADS, head, 0)
    finish_rows(mix[...], e_ref.at[tub - 1], wo_ref, out_vmem, out_hbm.at[tub - 1], sem).wait()


def finish_rows(mixed, e_ref, wo_ref, out_vmem, out_hbm, sem):
    product = jnp.dot(mixed.T, wo_ref[...], preferred_element_type=F32)
    out_vmem[...] = (e_ref[...].astype(F32) + product).astype(BF)
    store = pltpu.make_async_copy(out_vmem, out_hbm, sem)
    store.start()
    return store


def finish_kernel(w_ref, odd_ref, even_ref, ahead_ref, acc_ref, e_ref, wo_ref, _, out_hbm, far, mix, out_vmem, sem):
    count = far.shape[0]
    first, second = position()

    @pl.when(first)
    def _():
        far[...] = ahead_ref[1, 0:count]

    @pl.when(jnp.logical_not(first) & second)
    def _():
        far[...] = odd_ref[...]

    @pl.when(jnp.logical_not(first) & jnp.logical_not(second))
    def _():
        far[...] = even_ref[...]

    def head(h, carry):
        part = head_rows(h)
        values = [far[j, part, :].astype(F32) for j in range(count)]
        for t in range(count):
            total = acc_ref[t, part, :]
            for j in range(t, count):
                total = total + w_ref[t, j - t, pl.ds(h, 1), :] * values[j]
            mix[t, part, :] = total.astype(BF)
        return carry

    lax.fori_loop(0, HEADS, head, 0)
    stores = [
        finish_rows(mix[t], e_ref.at[t], wo_ref, out_vmem.at[t], out_hbm.at[t], sem.at[t])
        for t in range(count)
    ]
    for store in stores:
        store.wait()


def body(pixels, prior_kv, w_embed, ln_gain, w_query, w_key, w_value, w_out):
    tub, pat, pix = pixels.shape
    width, inner = w_query.shape
    rows, reach = tub * pat, 2 * tub
    count = lax.axis_size("tm")
    turned = (tub, inner, pat)
    most, rest = (tub - 1, inner, pat), (1, inner, pat)
    dma = pltpu.SemaphoreType.DMA

    def in_hbm(value):
        return pltpu.with_memory_space_constraint(value, pltpu.HBM)

    def ring(value):
        return lax.ppermute(value, "tm", [(i, (i + 2) % count) for i in range(count)])

    def shift(value, start=0, step=1):
        return lax.ppermute(value, "tm", [(i, i + 2) for i in range(start, count - 2, step)])

    def swap(value):
        return lax.ppermute(value, "tm", [(i, i ^ 1) for i in range(count)])

    pix_ahead = ring(pixels[tub - 1])
    embedded, normed, key_most, key_rest, w_embed, ln_gain, w_key, w_value, w_query, w_out = call(
        front_kernel, "front", 24,
        (
            shape((rows, width)), shape((rows, width)), shape(most), shape(rest),
            shape(w_embed.shape), shape(ln_gain.shape, F32), shape(w_key.shape),
            shape(w_value.shape), shape(w_query.shape), shape(w_out.shape),
        ),
        [HBM] * 7, (VMEM,) * 10,
        [pltpu.VMEM((rows, pix), BF), dma((4,)), dma((2,)), dma((3,))],
    )(
        in_hbm(pixels.reshape(rows, pix)), in_hbm(w_embed), in_hbm(ln_gain),
        in_hbm(w_key), in_hbm(w_value), in_hbm(w_query), in_hbm(w_out),
    )
    key_sent = ring(key_most)
    value_most, query, *value = call(
        second_kernel, "second", 16,
        (shape(most), shape(turned), *[shape((tub // V_PIECES, inner, pat))] * V_PIECES),
        [VMEM] * 3, (VMEM,) * (2 + V_PIECES),
    )(normed, w_value, w_query)
    value_swapped = [swap(part) for part in value]
    value_half = shift(
        call(
            pack_value_kernel, "pack_value", 16,
            shape((tub - 1, inner // 2, pat)), [VMEM] * (1 + V_PIECES), VMEM,
        )(value_most, *value_swapped)
    )
    value_even = shift(value_most, 0, 2)
    ahead, value_last = call(
        ahead_kernel, "ahead", 24,
        (shape((2, reach, inner, pat)), shape(rest)),
        [VMEM, HBM, VMEM, VMEM, VMEM, VMEM], (VMEM,) * 2,
        [pltpu.VMEM((pat, width), BF), pltpu.VMEM((2, reach, pat, inner), BF), dma((2,))],
    )(pix_ahead, in_hbm(prior_kv), w_embed, ln_gain, w_key, w_value)
    key_near = [
        swap(part)
        for part in call(
            pack_key_kernel, "pack_key", 16,
            (shape((tub // K_PIECES, inner, pat)),) * K_PIECES,
            [VMEM] * 4, (VMEM,) * K_PIECES,
        )(key_most, key_rest, key_sent, ahead)
    ]
    value_last = swap(value_last)
    weights = call(
        functools.partial(score_kernel, K_PIECES), "score", 16,
        shape((tub, reach + 1, HEADS, pat), F32),
        [VMEM] * (5 + K_PIECES), VMEM,
        [
            pltpu.VMEM((tub, reach + 1, HEADS, pat), F32), pltpu.VMEM(turned, BF),
            pltpu.VMEM(turned, BF),
        ],
    )(query, key_sent, ahead, *key_near, key_most, key_rest)
    value_other = swap(value_half)
    embedded = embedded.reshape(tub, pat, width)
    out, left, odd = call(
        functools.partial(mix_kernel, V_PIECES), "mix", 24,
        (shape((tub, pat, width)), shape(most, F32), shape(most)),
        [VMEM] * (7 + 2 * V_PIECES), (ANY, VMEM, VMEM),
        [pltpu.VMEM(turned, BF), pltpu.VMEM((inner, pat), BF), pltpu.VMEM((pat, width), BF), dma],
    )(weights, ahead, value_half, value_other, value_last, embedded, w_out, *value_swapped, *value)
    return call(
        finish_kernel, "finish", 24,
        shape((tub, pat, width)),
        [VMEM] * 7 + [ANY], ANY,
        [
            pltpu.VMEM(most, BF), pltpu.VMEM(most, BF), pltpu.VMEM((tub - 1, pat, width), BF),
            dma((tub,)),
        ],
        {7: 0},
    )(weights, odd, value_even, ahead, left, embedded, w_out, out)


def solution(mesh):
    placed = (
        P(("groups", "tm"), None, None),
        P(None, "groups", None, None),
        P(),
        P(),
        P(),
        P(),
        P(),
        P(),
    )
    return jax.shard_map(
        body, mesh=mesh, in_specs=placed, out_specs=P(("groups", "tm"), None, None), check_vma=False
    )
```

```python
import functools
import math

import jax
import jax.numpy as jnp
from jax import lax
from jax.experimental import pallas as pl
from jax.experimental.pallas import tpu as pltpu
from jax.sharding import PartitionSpec as P

HEADS = 8
HEAD_DIM = 80
BF = jnp.bfloat16
F32 = jnp.float32
ANY = pl.BlockSpec(memory_space=pl.ANY)
HBM = pl.BlockSpec(memory_space=pltpu.HBM)
VMEM = pl.BlockSpec(memory_space=pltpu.VMEM)
MIB = 1 << 20


def params(mib):
    return pltpu.CompilerParams(vmem_limit_bytes=mib * MIB)


COST = {"slice": 1, "front": 37000, "second": 1, "ahead": 1300, "pack_key": 1, "pack_value": 1,
        "score": 1, "mix": 1, "finish": 1}
K_PIECES = 2
V_PIECES = 2


def call(kernel, name, mib, out_shape, in_specs, out_specs, scratch=(), aliases=None):
    return pl.pallas_call(
        kernel,
        out_shape=out_shape,
        in_specs=in_specs,
        out_specs=out_specs,
        scratch_shapes=list(scratch),
        input_output_aliases=aliases or {},
        compiler_params=params(mib),
        cost_estimate=pl.CostEstimate(flops=COST[name] * 10**6, bytes_accessed=1, transcendentals=0),
        name=name,
    )


def shape(dims, dtype=BF):
    return jax.ShapeDtypeStruct(dims, dtype)


def head_rows(h):
    return pl.ds(pl.multiple_of(h * HEAD_DIM, 16), HEAD_DIM)


def normed_rows(emb, part, gain):
    wide = emb[part, :].astype(F32)
    center = wide - jnp.mean(wide, axis=-1, keepdims=True)
    spread = jnp.mean(center * center, axis=-1, keepdims=True)
    return (center * lax.rsqrt(spread + 1e-06) * gain).astype(BF)


def copy_in(pairs, sems):
    copies = [
        pltpu.make_async_copy(source, target, sems.at[i]) for i, (source, target) in enumerate(pairs)
    ]
    for copy in copies:
        copy.start()
    return copies


def position():
    place = lax.axis_index("tm")
    return place < 2, lax.rem(place, 2) == 1


def slice_kernel(pix_hbm, out_ref, sem):
    copy = pltpu.make_async_copy(pix_hbm.at[pix_hbm.shape[0] - 1], out_ref, sem)
    copy.start()
    copy.wait()


def front_kernel(pix_hbm, we_hbm, gain_hbm, wk_hbm, wv_hbm, wq_hbm, wo_hbm,
                 emb, nor, key_most, key_rest, we, gain_ref, wk, wv, wq, wo, pix, we_sem, sem, late_sem):
    rows, width = emb.shape
    tub = key_most.shape[0] + 1
    pat = rows // tub
    size, cut = rows // 2, width // 5 * 2
    parts = [slice(i * size, (i + 1) * size) for i in range(2)]
    halves = [slice(0, cut), slice(cut, width)]
    loads = copy_in(
        [
            (pix_hbm.at[pl.ds(0, size)], pix.at[pl.ds(0, size)]),
            (we_hbm.at[:, pl.ds(0, cut)], we.at[:, pl.ds(0, cut)]),
            (pix_hbm.at[pl.ds(size, size)], pix.at[pl.ds(size, size)]),
            (we_hbm.at[:, pl.ds(cut, width - cut)], we.at[:, pl.ds(cut, width - cut)]),
        ],
        we_sem,
    )
    more = copy_in([(gain_hbm, gain_ref), (wk_hbm, wk)], sem)
    for j, half in enumerate(halves):
        for i, part in enumerate(parts):
            if j == 0:
                loads[2 * i].wait()
            if i == 0:
                loads[1 + 2 * j].wait()
            if i == j == 1:
                later = copy_in([(wv_hbm, wv), (wq_hbm, wq), (wo_hbm, wo)], late_sem)
            emb[part, half] = jnp.dot(
                pix[part, :], we[:, half], preferred_element_type=F32
            ).astype(BF)
    more[0].wait()
    gain = gain_ref[...].reshape(1, width)
    for t in range(tub):
        part = slice(t * pat, (t + 1) * pat)
        nor[part, :] = normed_rows(emb, part, gain)
    more[1].wait()
    for i, part in enumerate(parts):
        product = jnp.dot(nor[part, :], wk[...], preferred_element_type=F32).astype(BF)
        for u in range(size // pat):
            t = i * (size // pat) + u
            turned = product[u * pat:(u + 1) * pat, :].T
            if t < tub - 1:
                key_most[t] = turned
            else:
                key_rest[0] = turned
    for load in later:
        load.wait()


def tubelets(refs):
    return [ref.at[t] for ref in refs for t in range(ref.shape[0])]


def second_kernel(nor, wv, wq, value_most, query, *values):
    tub, _, pat = query.shape
    size = nor.shape[0] // 2
    for weight, target in ((wv, tubelets(values)), (wq, tubelets([query]))):
        for i in range(2):
            product = jnp.dot(
                nor[i * size:(i + 1) * size, :], weight[...], preferred_element_type=F32
            ).astype(BF)
            for u in range(size // pat):
                t = i * (size // pat) + u
                turned = product[u * pat:(u + 1) * pat, :].T
                target[t][...] = turned
                if weight is wv and t < tub - 1:
                    value_most[t] = turned


def ahead_kernel(pix, prior_hbm, we, gain_ref, wk, wv, out, value_last, emb, held, sem):
    tub = out.shape[1] // 2
    pat = out.shape[3]
    first, second = position()

    @pl.when(first)
    def _():
        copies = copy_in([(prior_hbm.at[i], held.at[i]) for i in range(2)], sem)
        for i in range(2):
            copies[i].wait()
            for t in range(2 * tub):
                there = (t + second.astype(jnp.int32) * tub) % (2 * tub)
                out[i, t] = held[i, there].T

    @pl.when(jnp.logical_not(first))
    def _():
        emb[...] = jnp.dot(pix[...], we[...], preferred_element_type=F32).astype(BF)
        gain = gain_ref[...].reshape(1, emb.shape[1])
        nor = normed_rows(emb, slice(0, pat), gain)
        for i, weight in enumerate((wk, wv)):
            turned = jnp.dot(nor, weight[...], preferred_element_type=F32).astype(BF).T
            out[i, tub - 1] = turned
            if i == 1:
                value_last[0] = turned


def pack_key_kernel(most_ref, rest_ref, sent_ref, ahead_ref, *outs):
    tub = most_ref.shape[0] + 1
    size = tub // len(outs)
    _, second = position()
    for t in range(tub):
        out = outs[t // size].at[t % size]

        @pl.when(jnp.logical_not(second))
        def _():
            out[...] = most_ref[t] if t < tub - 1 else rest_ref[0]

        @pl.when(second)
        def _():
            out[...] = sent_ref[t] if t < tub - 1 else ahead_ref[0, t]


def pack_value_kernel(most_ref, *refs):
    *swapped_refs, out_ref = refs
    tub, half, _ = out_ref.shape
    _, second = position()

    @pl.when(jnp.logical_not(second))
    def _():
        for t, ref in enumerate(tubelets(swapped_refs)[:tub]):
            out_ref[t] = ref[0:half, :]

    @pl.when(second)
    def _():
        out_ref[...] = most_ref[:, half:, :]


def score_kernel(pieces, q_ref, sent_ref, ahead_ref, *refs):
    near_refs = refs[:pieces]
    most_ref, rest_ref, w_ref, s_ref, far_ref, near_ref = refs[pieces:]
    tub = q_ref.shape[0]
    reach = 2 * tub
    first, second = position()
    far_ref[tub - 1] = ahead_ref[0, tub - 1]

    @pl.when(first)
    def _():
        far_ref[0:tub - 1] = ahead_ref[0, 0:tub - 1]

    @pl.when(jnp.logical_not(first))
    def _():
        far_ref[0:tub - 1] = sent_ref[...]

    @pl.when(first & jnp.logical_not(second))
    def _():
        near_ref[...] = ahead_ref[0, tub:]

    @pl.when(jnp.logical_not(first) | second)
    def _():
        for t in range(tub):
            near_ref[t] = tubelets(near_refs)[t][...]

    keys = tubelets((far_ref, near_ref, most_ref, rest_ref))

    def head(h, carry):
        part = head_rows(h)
        queries = [q_ref[t, part, :].astype(F32) for t in range(tub)]
        for j in range(3 * tub):
            key = keys[j][part, :].astype(F32)
            for t in range(max(0, j - reach), min(j, tub - 1) + 1):
                s_ref[t, j - t, pl.ds(h, 1), :] = jnp.sum(queries[t] * key, axis=0, keepdims=True)
        return carry

    lax.fori_loop(0, HEADS, head, 0)
    scale = 1.0 / math.sqrt(HEAD_DIM)
    for t in range(tub):
        scores = [s_ref[t, j] * scale for j in range(reach + 1)]
        top = functools.reduce(jnp.maximum, scores)
        expo = [jnp.exp(s - top) for s in scores]
        total = functools.reduce(jnp.add, expo)
        for j in range(reach + 1):
            w_ref[t, j] = (expo[j] / total).astype(BF).astype(F32)


def mix_kernel(pieces, w_ref, ahead_ref, held_ref, other_ref, last_ref, e_ref, wo_ref, *refs):
    swapped, own = tubelets(refs[:pieces]), tubelets(refs[pieces:2 * pieces])
    out_hbm, acc_ref, odd_ref, near_ref, mix, out_vmem, sem = refs[2 * pieces:]
    tub = len(own)
    reach = 2 * tub
    half = held_ref.shape[1]
    first, second = position()

    @pl.when(second)
    def _():
        odd_ref[:, 0:half, :] = other_ref[...]
        odd_ref[:, half:, :] = held_ref[...]
        for t in range(tub):
            near_ref[t] = swapped[t][...]

    @pl.when(jnp.logical_not(second) & jnp.logical_not(first))
    def _():
        near_ref[0:tub - 1, 0:half, :] = held_ref[...]
        near_ref[0:tub - 1, half:, :] = other_ref[...]
        near_ref[tub - 1] = last_ref[0]

    @pl.when(jnp.logical_not(second) & first)
    def _():
        near_ref[...] = ahead_ref[1, tub:]

    values = [ahead_ref.at[1, tub - 1], *tubelets([near_ref]), *own]

    def head(h, carry):
        part = head_rows(h)
        sums = [None] * tub
        for j in range(tub - 1, 3 * tub):
            value = values[j - tub + 1][part, :].astype(F32)
            for t in range(max(0, j - reach), min(j, tub - 1) + 1):
                term = w_ref[t, j - t, pl.ds(h, 1), :] * value
                sums[t] = term if sums[t] is None else sums[t] + term
        for t in range(tub - 1):
            acc_ref[t, part, :] = sums[t]
        mix[part, :] = sums[tub - 1].astype(BF)
        return carry

    lax.fori_loop(0, HEADS, head, 0)
    finish_rows(mix[...], e_ref.at[tub - 1], wo_ref, out_vmem, out_hbm.at[tub - 1], sem).wait()


def finish_rows(mixed, e_ref, wo_ref, out_vmem, out_hbm, sem):
    product = jnp.dot(mixed.T, wo_ref[...], preferred_element_type=F32)
    out_vmem[...] = (e_ref[...].astype(F32) + product).astype(BF)
    store = pltpu.make_async_copy(out_vmem, out_hbm, sem)
    store.start()
    return store


def finish_kernel(w_ref, odd_ref, even_ref, ahead_ref, acc_ref, e_ref, wo_ref, _, out_hbm, far, out_vmem, sem):
    count = far.shape[0]
    first, second = position()

    @pl.when(first)
    def _():
        far[...] = ahead_ref[1, 0:count]

    @pl.when(jnp.logical_not(first) & second)
    def _():
        far[...] = odd_ref[...]

    @pl.when(jnp.logical_not(first) & jnp.logical_not(second))
    def _():
        far[...] = even_ref[...]

    stores = []
    for t in reversed(range(count)):
        heads = []
        for h in range(HEADS):
            part = slice(h * HEAD_DIM, (h + 1) * HEAD_DIM)
            total = acc_ref[t, part, :]
            for j in range(t, count):
                total = total + w_ref[t, j - t, h:h + 1, :] * far[j, part, :].astype(F32)
            heads.append(total.astype(BF))
        mixed = jnp.concatenate(heads, axis=0)
        stores.append(
            finish_rows(mixed, e_ref.at[t], wo_ref, out_vmem.at[t], out_hbm.at[t], sem.at[t])
        )
    for store in stores:
        store.wait()


def body(pixels, prior_kv, w_embed, ln_gain, w_query, w_key, w_value, w_out):
    tub, pat, pix = pixels.shape
    width, inner = w_query.shape
    rows, reach = tub * pat, 2 * tub
    count = lax.axis_size("tm")
    turned = (tub, inner, pat)
    most, rest = (tub - 1, inner, pat), (1, inner, pat)
    dma = pltpu.SemaphoreType.DMA

    def in_hbm(value):
        return pltpu.with_memory_space_constraint(value, pltpu.HBM)

    def ring(value):
        return lax.ppermute(value, "tm", [(i, (i + 2) % count) for i in range(count)])

    def shift(value, start=0, step=1):
        return lax.ppermute(value, "tm", [(i, i + 2) for i in range(start, count - 2, step)])

    def swap(value):
        return lax.ppermute(value, "tm", [(i, i ^ 1) for i in range(count)])

    pix_ahead = ring(
        call(
            slice_kernel, "slice", 16, shape((pat, pix)), [HBM], VMEM, [dma]
        )(in_hbm(pixels))
    )
    embedded, normed, key_most, key_rest, w_embed, ln_gain, w_key, w_value, w_query, w_out = call(
        front_kernel, "front", 24,
        (
            shape((rows, width)), shape((rows, width)), shape(most), shape(rest),
            shape(w_embed.shape), shape(ln_gain.shape, F32), shape(w_key.shape),
            shape(w_value.shape), shape(w_query.shape), shape(w_out.shape),
        ),
        [HBM] * 7, (VMEM,) * 10,
        [pltpu.VMEM((rows, pix), BF), dma((4,)), dma((2,)), dma((3,))],
    )(
        in_hbm(pixels.reshape(rows, pix)), in_hbm(w_embed), in_hbm(ln_gain),
        in_hbm(w_key), in_hbm(w_value), in_hbm(w_query), in_hbm(w_out),
    )
    key_sent = ring(key_most)
    value_most, query, *value = call(
        second_kernel, "second", 16,
        (shape(most), shape(turned), *[shape((tub // V_PIECES, inner, pat))] * V_PIECES),
        [VMEM] * 3, (VMEM,) * (2 + V_PIECES),
    )(normed, w_value, w_query)
    value_swapped = [swap(part) for part in value]
    value_half = shift(
        call(
            pack_value_kernel, "pack_value", 16,
            shape((tub - 1, inner // 2, pat)), [VMEM] * (1 + V_PIECES), VMEM,
        )(value_most, *value_swapped)
    )
    value_even = shift(value_most, 0, 2)
    ahead, value_last = call(
        ahead_kernel, "ahead", 24,
        (shape((2, reach, inner, pat)), shape(rest)),
        [VMEM, HBM, VMEM, VMEM, VMEM, VMEM], (VMEM,) * 2,
        [pltpu.VMEM((pat, width), BF), pltpu.VMEM((2, reach, pat, inner), BF), dma((2,))],
    )(pix_ahead, in_hbm(prior_kv), w_embed, ln_gain, w_key, w_value)
    key_near = [
        swap(part)
        for part in call(
            pack_key_kernel, "pack_key", 16,
            (shape((tub // K_PIECES, inner, pat)),) * K_PIECES,
            [VMEM] * 4, (VMEM,) * K_PIECES,
        )(key_most, key_rest, key_sent, ahead)
    ]
    value_last = swap(value_last)
    weights = call(
        functools.partial(score_kernel, K_PIECES), "score", 16,
        shape((tub, reach + 1, HEADS, pat), F32),
        [VMEM] * (5 + K_PIECES), VMEM,
        [
            pltpu.VMEM((tub, reach + 1, HEADS, pat), F32), pltpu.VMEM(turned, BF),
            pltpu.VMEM(turned, BF),
        ],
    )(query, key_sent, ahead, *key_near, key_most, key_rest)
    value_other = swap(value_half)
    embedded = embedded.reshape(tub, pat, width)
    out, left, odd = call(
        functools.partial(mix_kernel, V_PIECES), "mix", 24,
        (shape((tub, pat, width)), shape(most, F32), shape(most)),
        [VMEM] * (7 + 2 * V_PIECES), (ANY, VMEM, VMEM),
        [pltpu.VMEM(turned, BF), pltpu.VMEM((inner, pat), BF), pltpu.VMEM((pat, width), BF), dma],
    )(weights, ahead, value_half, value_other, value_last, embedded, w_out, *value_swapped, *value)
    return call(
        finish_kernel, "finish", 24,
        shape((tub, pat, width)),
        [VMEM] * 7 + [ANY], ANY,
        [
            pltpu.VMEM(most, BF), pltpu.VMEM((tub - 1, pat, width), BF), dma((tub - 1,)),
        ],
        {7: 0},
    )(weights, odd, value_even, ahead, left, embedded, w_out, out)


def solution(mesh):
    placed = (
        P(("groups", "tm"), None, None),
        P(None, "groups", None, None),
        P(),
        P(),
        P(),
        P(),
        P(),
        P(),
    )
    return jax.shard_map(
        body, mesh=mesh, in_specs=placed, out_specs=P(("groups", "tm"), None, None), check_vma=False
    )
```

```python
import functools
import math

import jax
import jax.numpy as jnp
from jax import lax
from jax.experimental import pallas as pl
from jax.experimental.pallas import tpu as pltpu
from jax.sharding import PartitionSpec as P

HEADS = 8
HEAD_DIM = 80
BF = jnp.bfloat16
F32 = jnp.float32
ANY = pl.BlockSpec(memory_space=pl.ANY)
HBM = pl.BlockSpec(memory_space=pltpu.HBM)
VMEM = pl.BlockSpec(memory_space=pltpu.VMEM)
MIB = 1 << 20


def params(mib):
    return pltpu.CompilerParams(vmem_limit_bytes=mib * MIB)


COST = {"slice": 1, "front": 37000, "second": 1, "ahead": 1300, "pack_key": 1000, "pack_value": 1,
        "score": 1, "weight": 1, "mix": 1, "finish": 1}
K_PIECES = 2
V_PIECES = 2
R_PIECES = 2


def call(kernel, name, mib, out_shape, in_specs, out_specs, scratch=(), aliases=None):
    return pl.pallas_call(
        kernel,
        out_shape=out_shape,
        in_specs=in_specs,
        out_specs=out_specs,
        scratch_shapes=list(scratch),
        input_output_aliases=aliases or {},
        compiler_params=params(mib),
        cost_estimate=pl.CostEstimate(flops=COST[name] * 10**6, bytes_accessed=1, transcendentals=0),
        name=name,
    )


def shape(dims, dtype=BF):
    return jax.ShapeDtypeStruct(dims, dtype)


def head_rows(h):
    return pl.ds(pl.multiple_of(h * HEAD_DIM, 16), HEAD_DIM)


def normed_rows(emb, part, gain):
    wide = emb[part, :].astype(F32)
    center = wide - jnp.mean(wide, axis=-1, keepdims=True)
    spread = jnp.mean(center * center, axis=-1, keepdims=True)
    return (center * lax.rsqrt(spread + 1e-06) * gain).astype(BF)


def copy_in(pairs, sems):
    copies = [
        pltpu.make_async_copy(source, target, sems.at[i]) for i, (source, target) in enumerate(pairs)
    ]
    for copy in copies:
        copy.start()
    return copies


def position():
    place = lax.axis_index("tm")
    return place < 2, lax.rem(place, 2) == 1


def slice_kernel(pix_hbm, out_ref, sem):
    copy = pltpu.make_async_copy(pix_hbm.at[pix_hbm.shape[0] - 1], out_ref, sem)
    copy.start()
    copy.wait()


def front_kernel(pix_hbm, we_hbm, gain_hbm, wk_hbm, wv_hbm, wq_hbm, wo_hbm,
                 emb, nor, key_most, key_rest, we, gain_ref, wk, wv, wq, wo, pix, we_sem, sem, late_sem):
    rows, width = emb.shape
    tub = key_most.shape[0] + 1
    pat = rows // tub
    size, cut = rows // 2, width // 5 * 2
    parts = [slice(i * size, (i + 1) * size) for i in range(2)]
    halves = [slice(0, cut), slice(cut, width)]
    loads = copy_in(
        [
            (pix_hbm.at[pl.ds(0, size)], pix.at[pl.ds(0, size)]),
            (we_hbm.at[:, pl.ds(0, cut)], we.at[:, pl.ds(0, cut)]),
            (pix_hbm.at[pl.ds(size, size)], pix.at[pl.ds(size, size)]),
            (we_hbm.at[:, pl.ds(cut, width - cut)], we.at[:, pl.ds(cut, width - cut)]),
        ],
        we_sem,
    )
    more = copy_in([(gain_hbm, gain_ref), (wk_hbm, wk)], sem)
    for j, half in enumerate(halves):
        for i, part in enumerate(parts):
            if j == 0:
                loads[2 * i].wait()
            if i == 0:
                loads[1 + 2 * j].wait()
            if i == j == 1:
                later = copy_in([(wv_hbm, wv), (wq_hbm, wq), (wo_hbm, wo)], late_sem)
            emb[part, half] = jnp.dot(
                pix[part, :], we[:, half], preferred_element_type=F32
            ).astype(BF)
    more[0].wait()
    gain = gain_ref[...].reshape(1, width)
    for t in range(tub):
        part = slice(t * pat, (t + 1) * pat)
        nor[part, :] = normed_rows(emb, part, gain)
    more[1].wait()
    for i, part in enumerate(parts):
        product = jnp.dot(nor[part, :], wk[...], preferred_element_type=F32).astype(BF)
        for u in range(size // pat):
            t = i * (size // pat) + u
            turned = product[u * pat:(u + 1) * pat, :].T
            if t < tub - 1:
                key_most[t] = turned
            else:
                key_rest[0] = turned
    for load in later:
        load.wait()


def tubelets(refs):
    return [ref.at[t] for ref in refs for t in range(ref.shape[0])]


def second_kernel(nor, wv, wq, value_start, query, *values):
    tub, _, pat = query.shape
    size = nor.shape[0] // 2
    for weight, target in ((wv, tubelets(values)), (wq, tubelets([query]))):
        for i in range(2):
            product = jnp.dot(
                nor[i * size:(i + 1) * size, :], weight[...], preferred_element_type=F32
            ).astype(BF)
            for u in range(size // pat):
                t = i * (size // pat) + u
                turned = product[u * pat:(u + 1) * pat, :].T
                target[t][...] = turned
                if weight is wv and t < value_start.shape[0]:
                    value_start[t] = turned


def ahead_kernel(pix, prior_hbm, we, gain_ref, wk, wv, out, value_last, emb, held, sem):
    tub = out.shape[1] // 2
    pat = out.shape[3]
    first, second = position()

    @pl.when(first)
    def _():
        copies = copy_in([(prior_hbm.at[i], held.at[i]) for i in range(2)], sem)
        for i in range(2):
            copies[i].wait()
            for t in range(2 * tub):
                there = (t + second.astype(jnp.int32) * tub) % (2 * tub)
                out[i, t] = held[i, there].T

    @pl.when(jnp.logical_not(first))
    def _():
        emb[...] = jnp.dot(pix[...], we[...], preferred_element_type=F32).astype(BF)
        gain = gain_ref[...].reshape(1, emb.shape[1])
        nor = normed_rows(emb, slice(0, pat), gain)
        for i, weight in enumerate((wk, wv)):
            turned = jnp.dot(nor, weight[...], preferred_element_type=F32).astype(BF).T
            out[i, tub - 1] = turned
            if i == 1:
                value_last[0] = turned


def pack_key_kernel(most_ref, rest_ref, sent_ref, ahead_ref, *outs):
    tub = most_ref.shape[0] + 1
    size = tub // len(outs)
    _, second = position()
    for t in range(tub):
        out = outs[t // size].at[t % size]

        @pl.when(jnp.logical_not(second))
        def _():
            out[...] = most_ref[t] if t < tub - 1 else rest_ref[0]

        @pl.when(second)
        def _():
            out[...] = sent_ref[t] if t < tub - 1 else ahead_ref[0, t]


def pack_value_kernel(pieces, *refs):
    own, swapped, out_ref = tubelets(refs[:pieces]), tubelets(refs[pieces:2 * pieces]), refs[2 * pieces]
    tub, half, _ = out_ref.shape
    _, second = position()

    @pl.when(jnp.logical_not(second))
    def _():
        for t in range(tub - 1):
            out_ref[t] = swapped[t][0:half, :]
        out_ref[tub - 1] = own[tub - 2][0:half, :]

    @pl.when(second)
    def _():
        for t in range(tub - 1):
            out_ref[t] = own[t][half:, :]
        out_ref[tub - 1] = swapped[tub - 2][half:, :]


def scored(blocks, q_ref, s_ref):
    tub = q_ref.shape[0]
    reach = 2 * tub

    def head(h, carry):
        part = head_rows(h)
        queries = [q_ref[t, part, :].astype(F32) for t in range(tub)]
        for j, key_ref in blocks.items():
            key = key_ref[part, :].astype(F32)
            for t in range(max(0, j - reach), min(j, tub - 1) + 1):
                s_ref[t, j - t, pl.ds(h, 1), :] = jnp.sum(queries[t] * key, axis=0, keepdims=True)
        return carry

    lax.fori_loop(0, HEADS, head, 0)


def score_kernel(q_ref, sent_ref, ahead_ref, most_ref, rest_ref, s_ref, far_ref):
    tub = q_ref.shape[0]
    first, _ = position()
    far_ref[tub - 1] = ahead_ref[0, tub - 1]

    @pl.when(first)
    def _():
        far_ref[0:tub - 1] = ahead_ref[0, 0:tub - 1]

    @pl.when(jnp.logical_not(first))
    def _():
        far_ref[0:tub - 1] = sent_ref[...]

    keys = tubelets([far_ref]) + [None] * tub + tubelets((most_ref, rest_ref))
    scored({j: key for j, key in enumerate(keys) if key is not None}, q_ref, s_ref)


def weight_kernel(pieces, q_ref, ahead_ref, far_own_ref, *refs):
    near_refs = refs[:pieces]
    w_ref, s_ref, near_ref = refs[pieces:]
    tub = q_ref.shape[0]
    reach = 2 * tub
    first, second = position()

    @pl.when(first & jnp.logical_not(second))
    def _():
        near_ref[...] = ahead_ref[0, tub:]

    @pl.when(jnp.logical_not(first) | second)
    def _():
        for t in range(tub):
            near_ref[t] = tubelets(near_refs)[t][...]

    scored({tub + j: near_ref.at[j] for j in range(tub)}, q_ref, s_ref)
    scale = 1.0 / math.sqrt(HEAD_DIM)
    for t in range(tub):
        scores = [
            (s_ref if tub <= t + d < reach else far_own_ref)[t, d] * scale for d in range(reach + 1)
        ]
        top = functools.reduce(jnp.maximum, scores)
        expo = [jnp.exp(s - top) for s in scores]
        total = functools.reduce(jnp.add, expo)
        for d in range(reach + 1):
            w_ref[t, d] = (expo[d] / total).astype(BF).astype(F32)


def mix_kernel(pieces, other_pieces, w_ref, ahead_ref, held_ref, last_ref, e_ref, wo_ref, *refs):
    others, refs = refs[:other_pieces], refs[other_pieces:]
    swapped, own = tubelets(refs[:pieces]), tubelets(refs[pieces:2 * pieces])
    done_ref, acc_ref, odd_ref, near_ref, far_ref, mix = refs[2 * pieces:]
    tub = len(own)
    reach, start = 2 * tub, acc_ref.shape[0]
    half = held_ref.shape[1]
    first, second = position()

    def join(target, tubelet, low):
        target[(slice(0, half) if low else slice(half, 2 * half)), :] = held_ref[tubelet]
        for i, ref in enumerate(others):
            size = ref.shape[1]
            place = i * size + (half if low else 0)
            target[place:place + size, :] = ref[tubelet]

    @pl.when(second)
    def _():
        for t in range(start):
            join(odd_ref.at[t], t, False)
        for t in range(tub):
            near_ref[t] = swapped[t][...]

    @pl.when(second & jnp.logical_not(first))
    def _():
        join(far_ref, start, False)

    @pl.when(jnp.logical_not(second) & jnp.logical_not(first))
    def _():
        for t in range(tub - 1):
            join(near_ref.at[t], t, True)
        near_ref[tub - 1] = last_ref[0]
        join(far_ref, tub - 1, True)

    @pl.when(first)
    def _():
        far_ref[...] = ahead_ref[1, start]

    @pl.when(jnp.logical_not(second) & first)
    def _():
        near_ref[...] = ahead_ref[1, tub:]

    values = [far_ref, ahead_ref.at[1, tub - 1], *tubelets([near_ref]), *own]

    def head(h, carry):
        part = head_rows(h)
        sums = [None] * tub
        for j in range(start, 3 * tub):
            value = values[j - start][part, :].astype(F32)
            for t in range(max(0, j - reach), min(j, tub - 1) + 1):
                term = w_ref[t, j - t, pl.ds(h, 1), :] * value
                sums[t] = term if sums[t] is None else sums[t] + term
        for t in range(tub):
            if t < start:
                acc_ref[t, part, :] = sums[t]
            else:
                mix[t - start, part, :] = sums[t].astype(BF)
        return carry

    lax.fori_loop(0, HEADS, head, 0)
    for t in range(start, tub):
        done_ref[t - start] = finished(mix[t - start], e_ref.at[t], wo_ref)


def finished(mixed, e_ref, wo_ref):
    product = jnp.dot(mixed.T, wo_ref[...], preferred_element_type=F32)
    return (e_ref[...].astype(F32) + product).astype(BF)


def finish_kernel(w_ref, odd_ref, even_ref, ahead_ref, acc_ref, e_ref, wo_ref, done_ref,
                  out_hbm, far, out_vmem, sem):
    count = far.shape[0]
    first, second = position()
    written = pltpu.make_async_copy(done_ref, out_hbm.at[pl.ds(count, done_ref.shape[0])], sem.at[count])
    written.start()

    @pl.when(first)
    def _():
        far[...] = ahead_ref[1, 0:count]

    @pl.when(jnp.logical_not(first) & second)
    def _():
        far[...] = odd_ref[...]

    @pl.when(jnp.logical_not(first) & jnp.logical_not(second))
    def _():
        far[...] = even_ref[...]

    stores = [written]
    for t in reversed(range(count)):
        heads = []
        for h in range(HEADS):
            part = slice(h * HEAD_DIM, (h + 1) * HEAD_DIM)
            total = acc_ref[t, part, :]
            for j in range(t, count):
                total = total + w_ref[t, j - t, h:h + 1, :] * far[j, part, :].astype(F32)
            heads.append(total.astype(BF))
        out_vmem[t] = finished(jnp.concatenate(heads, axis=0), e_ref.at[t], wo_ref)
        stores.append(pltpu.make_async_copy(out_vmem.at[t], out_hbm.at[t], sem.at[t]))
        stores[-1].start()
    for store in stores:
        store.wait()


def body(pixels, prior_kv, w_embed, ln_gain, w_query, w_key, w_value, w_out):
    tub, pat, pix = pixels.shape
    width, inner = w_query.shape
    rows, reach = tub * pat, 2 * tub
    count = lax.axis_size("tm")
    turned = (tub, inner, pat)
    most, rest, start = (tub - 1, inner, pat), (1, inner, pat), (tub - 2, inner, pat)
    dma = pltpu.SemaphoreType.DMA

    def in_hbm(value):
        return pltpu.with_memory_space_constraint(value, pltpu.HBM)

    def ring(value):
        return lax.ppermute(value, "tm", [(i, (i + 2) % count) for i in range(count)])

    def shift(value, start=0, step=1):
        return lax.ppermute(value, "tm", [(i, i + 2) for i in range(start, count - 2, step)])

    def swap(value):
        return lax.ppermute(value, "tm", [(i, i ^ 1) for i in range(count)])

    pix_ahead = ring(
        call(
            slice_kernel, "slice", 16, shape((pat, pix)), [HBM], VMEM, [dma]
        )(in_hbm(pixels))
    )
    embedded, normed, key_most, key_rest, w_embed, ln_gain, w_key, w_value, w_query, w_out = call(
        front_kernel, "front", 24,
        (
            shape((rows, width)), shape((rows, width)), shape(most), shape(rest),
            shape(w_embed.shape), shape(ln_gain.shape, F32), shape(w_key.shape),
            shape(w_value.shape), shape(w_query.shape), shape(w_out.shape),
        ),
        [HBM] * 7, (VMEM,) * 10,
        [pltpu.VMEM((rows, pix), BF), dma((4,)), dma((2,)), dma((3,))],
    )(
        in_hbm(pixels.reshape(rows, pix)), in_hbm(w_embed), in_hbm(ln_gain),
        in_hbm(w_key), in_hbm(w_value), in_hbm(w_query), in_hbm(w_out),
    )
    key_sent = ring(key_most)
    value_start, query, *value = call(
        second_kernel, "second", 16,
        (shape(start), shape(turned), *[shape((tub // V_PIECES, inner, pat))] * V_PIECES),
        [VMEM] * 3, (VMEM,) * (2 + V_PIECES),
    )(normed, w_value, w_query)
    value_swapped = [swap(part) for part in value]
    value_half = shift(
        call(
            functools.partial(pack_value_kernel, V_PIECES), "pack_value", 16,
            shape((tub, inner // 2, pat)), [VMEM] * (2 * V_PIECES), VMEM,
        )(*value, *value_swapped)
    )
    value_even = shift(value_start, 0, 2)
    ahead, value_last = call(
        ahead_kernel, "ahead", 24,
        (shape((2, reach, inner, pat)), shape(rest)),
        [VMEM, HBM, VMEM, VMEM, VMEM, VMEM], (VMEM,) * 2,
        [pltpu.VMEM((pat, width), BF), pltpu.VMEM((2, reach, pat, inner), BF), dma((2,))],
    )(pix_ahead, in_hbm(prior_kv), w_embed, ln_gain, w_key, w_value)
    scores = call(
        score_kernel, "score", 16,
        shape((tub, reach + 1, HEADS, pat), F32),
        [VMEM] * 5, VMEM, [pltpu.VMEM(turned, BF)],
    )(query, key_sent, ahead, key_most, key_rest)
    key_near = [
        swap(part)
        for part in call(
            pack_key_kernel, "pack_key", 16,
            (shape((tub // K_PIECES, inner, pat)),) * K_PIECES,
            [VMEM] * 4, (VMEM,) * K_PIECES,
        )(key_most, key_rest, key_sent, ahead)
    ]
    value_last, scores = lax.optimization_barrier((value_last, scores))
    value_last = swap(value_last)
    weights = call(
        functools.partial(weight_kernel, K_PIECES), "weight", 16,
        shape((tub, reach + 1, HEADS, pat), F32),
        [VMEM] * (3 + K_PIECES), VMEM,
        [pltpu.VMEM((tub, reach + 1, HEADS, pat), F32), pltpu.VMEM(turned, BF)],
    )(query, ahead, scores, *key_near)
    cut = inner // 2 // R_PIECES
    value_other = [swap(value_half[:, i * cut:(i + 1) * cut, :]) for i in range(R_PIECES)]
    embedded = embedded.reshape(tub, pat, width)
    done, left, odd = call(
        functools.partial(mix_kernel, V_PIECES, R_PIECES), "mix", 24,
        (shape((2, pat, width)), shape(start, F32), shape(start)),
        [VMEM] * (6 + R_PIECES + 2 * V_PIECES), (VMEM,) * 3,
        [pltpu.VMEM(turned, BF), pltpu.VMEM((inner, pat), BF), pltpu.VMEM((2, inner, pat), BF)],
    )(weights, ahead, value_half, value_last, embedded, w_out, *value_other, *value_swapped, *value)
    return call(
        finish_kernel, "finish", 24,
        shape((tub, pat, width)),
        [VMEM] * 8, ANY,
        [
            pltpu.VMEM(start, BF), pltpu.VMEM((tub - 2, pat, width), BF), dma((tub - 1,)),
        ],
    )(weights, odd, value_even, ahead, left, embedded, w_out, done)


def solution(mesh):
    placed = (
        P(("groups", "tm"), None, None),
        P(None, "groups", None, None),
        P(),
        P(),
        P(),
        P(),
        P(),
        P(),
    )
    return jax.shard_map(
        body, mesh=mesh, in_specs=placed, out_specs=P(("groups", "tm"), None, None), check_vma=False
    )
```

```python
import functools
import math

import jax
import jax.numpy as jnp
from jax import lax
from jax.experimental import pallas as pl
from jax.experimental.pallas import tpu as pltpu
from jax.sharding import PartitionSpec as P

HEADS = 8
HEAD_DIM = 80
BF = jnp.bfloat16
F32 = jnp.float32
ANY = pl.BlockSpec(memory_space=pl.ANY)
HBM = pl.BlockSpec(memory_space=pltpu.HBM)
VMEM = pl.BlockSpec(memory_space=pltpu.VMEM)
MIB = 1 << 20


def params(mib):
    return pltpu.CompilerParams(vmem_limit_bytes=mib * MIB)


COST = {"slice": 1, "front": 37000, "second": 1, "ahead": 1300, "pack_key": 1000, "pack_value": 1,
        "score": 1, "weight": 1, "mix": 1, "finish": 1}
K_PIECES = 2
V_PIECES = 2
R_PIECES = 2


def call(kernel, name, mib, out_shape, in_specs, out_specs, scratch=(), aliases=None):
    return pl.pallas_call(
        kernel,
        out_shape=out_shape,
        in_specs=in_specs,
        out_specs=out_specs,
        scratch_shapes=list(scratch),
        input_output_aliases=aliases or {},
        compiler_params=params(mib),
        cost_estimate=pl.CostEstimate(flops=COST[name] * 10**6, bytes_accessed=1, transcendentals=0),
        name=name,
    )


def shape(dims, dtype=BF):
    return jax.ShapeDtypeStruct(dims, dtype)


def head_rows(h):
    return pl.ds(pl.multiple_of(h * HEAD_DIM, 16), HEAD_DIM)


def normed_rows(emb, part, gain):
    wide = emb[part, :].astype(F32)
    center = wide - jnp.mean(wide, axis=-1, keepdims=True)
    spread = jnp.mean(center * center, axis=-1, keepdims=True)
    return (center * lax.rsqrt(spread + 1e-06) * gain).astype(BF)


def copy_in(pairs, sems):
    copies = [
        pltpu.make_async_copy(source, target, sems.at[i]) for i, (source, target) in enumerate(pairs)
    ]
    for copy in copies:
        copy.start()
    return copies


def position():
    place = lax.axis_index("tm")
    return place < 2, lax.rem(place, 2) == 1


def slice_kernel(pix_hbm, out_ref, sem):
    copy = pltpu.make_async_copy(pix_hbm.at[pix_hbm.shape[0] - 1], out_ref, sem)
    copy.start()
    copy.wait()


def front_kernel(pix_hbm, we_hbm, gain_hbm, wk_hbm, wv_hbm, wq_hbm, wo_hbm,
                 emb, nor, key_most, key_rest, we, gain_ref, wk, wv, wq, wo, pix, we_sem, sem, late_sem):
    rows, width = emb.shape
    tub = key_most.shape[0] + 1
    pat = rows // tub
    size, cut = rows // 2, width // 5 * 2
    parts = [slice(i * size, (i + 1) * size) for i in range(2)]
    halves = [slice(0, cut), slice(cut, width)]
    loads = copy_in(
        [
            (pix_hbm.at[pl.ds(0, size)], pix.at[pl.ds(0, size)]),
            (we_hbm.at[:, pl.ds(0, cut)], we.at[:, pl.ds(0, cut)]),
            (pix_hbm.at[pl.ds(size, size)], pix.at[pl.ds(size, size)]),
            (we_hbm.at[:, pl.ds(cut, width - cut)], we.at[:, pl.ds(cut, width - cut)]),
        ],
        we_sem,
    )
    more = copy_in([(gain_hbm, gain_ref), (wk_hbm, wk)], sem)
    for j, half in enumerate(halves):
        for i, part in enumerate(parts):
            if j == 0:
                loads[2 * i].wait()
            if i == 0:
                loads[1 + 2 * j].wait()
            if i == j == 1:
                later = copy_in([(wv_hbm, wv), (wq_hbm, wq), (wo_hbm, wo)], late_sem)
            emb[part, half] = jnp.dot(
                pix[part, :], we[:, half], preferred_element_type=F32
            ).astype(BF)
    more[0].wait()
    gain = gain_ref[...].reshape(1, width)
    for t in range(tub):
        part = slice(t * pat, (t + 1) * pat)
        nor[part, :] = normed_rows(emb, part, gain)
    more[1].wait()
    for i, part in enumerate(parts):
        product = jnp.dot(nor[part, :], wk[...], preferred_element_type=F32).astype(BF)
        for u in range(size // pat):
            t = i * (size // pat) + u
            turned = product[u * pat:(u + 1) * pat, :].T
            if t < tub - 1:
                key_most[t] = turned
            else:
                key_rest[0] = turned
    for load in later:
        load.wait()


def tubelets(refs):
    return [ref.at[t] for ref in refs for t in range(ref.shape[0])]


def second_kernel(nor, wv, wq, value_start, query, *values):
    tub, _, pat = query.shape
    size = nor.shape[0] // 2
    for weight, target in ((wv, tubelets(values)), (wq, tubelets([query]))):
        for i in range(2):
            product = jnp.dot(
                nor[i * size:(i + 1) * size, :], weight[...], preferred_element_type=F32
            ).astype(BF)
            for u in range(size // pat):
                t = i * (size // pat) + u
                turned = product[u * pat:(u + 1) * pat, :].T
                target[t][...] = turned
                if weight is wv and t < value_start.shape[0]:
                    value_start[t] = turned


def ahead_kernel(pix, prior_hbm, we, gain_ref, wk, wv, out, value_last, emb, held, sem):
    tub = out.shape[1] // 2
    pat = out.shape[3]
    first, second = position()

    @pl.when(first)
    def _():
        copies = copy_in([(prior_hbm.at[i], held.at[i]) for i in range(2)], sem)
        for i in range(2):
            copies[i].wait()
            for t in range(2 * tub):
                there = (t + second.astype(jnp.int32) * tub) % (2 * tub)
                out[i, t] = held[i, there].T

    @pl.when(jnp.logical_not(first))
    def _():
        emb[...] = jnp.dot(pix[...], we[...], preferred_element_type=F32).astype(BF)
        gain = gain_ref[...].reshape(1, emb.shape[1])
        nor = normed_rows(emb, slice(0, pat), gain)
        for i, weight in enumerate((wk, wv)):
            turned = jnp.dot(nor, weight[...], preferred_element_type=F32).astype(BF).T
            out[i, tub - 1] = turned
            if i == 1:
                value_last[0] = turned


def pack_key_kernel(most_ref, rest_ref, sent_ref, ahead_ref, *outs):
    tub = most_ref.shape[0] + 1
    size = tub // len(outs)
    _, second = position()
    for t in range(tub):
        out = outs[t // size].at[t % size]

        @pl.when(jnp.logical_not(second))
        def _():
            out[...] = most_ref[t] if t < tub - 1 else rest_ref[0]

        @pl.when(second)
        def _():
            out[...] = sent_ref[t] if t < tub - 1 else ahead_ref[0, t]


def pack_value_kernel(pieces, *refs):
    own, swapped, out_ref = tubelets(refs[:pieces]), tubelets(refs[pieces:2 * pieces]), refs[2 * pieces]
    tub, half, _ = out_ref.shape
    _, second = position()

    @pl.when(jnp.logical_not(second))
    def _():
        for t in range(tub - 1):
            out_ref[t] = swapped[t][0:half, :]
        out_ref[tub - 1] = own[tub - 2][0:half, :]

    @pl.when(second)
    def _():
        for t in range(tub - 1):
            out_ref[t] = own[t][half:, :]
        out_ref[tub - 1] = swapped[tub - 2][half:, :]


def scored(blocks, q_ref, s_ref):
    tub = q_ref.shape[0]
    reach = 2 * tub

    def head(h, carry):
        part = head_rows(h)
        queries = [q_ref[t, part, :].astype(F32) for t in range(tub)]
        for j, key_ref in blocks.items():
            key = key_ref[part, :].astype(F32)
            for t in range(max(0, j - reach), min(j, tub - 1) + 1):
                s_ref[t, j - t, pl.ds(h, 1), :] = jnp.sum(queries[t] * key, axis=0, keepdims=True)
        return carry

    lax.fori_loop(0, HEADS, head, 0)


def score_kernel(q_ref, sent_ref, ahead_ref, most_ref, rest_ref, s_ref, far_ref):
    tub = q_ref.shape[0]
    first, _ = position()
    far_ref[tub - 1] = ahead_ref[0, tub - 1]

    @pl.when(first)
    def _():
        far_ref[0:tub - 1] = ahead_ref[0, 0:tub - 1]

    @pl.when(jnp.logical_not(first))
    def _():
        far_ref[0:tub - 1] = sent_ref[...]

    keys = tubelets([far_ref]) + [None] * tub + tubelets((most_ref, rest_ref))
    scored({j: key for j, key in enumerate(keys) if key is not None}, q_ref, s_ref)


def weight_kernel(pieces, q_ref, ahead_ref, far_own_ref, *refs):
    near_refs = refs[:pieces]
    w_ref, s_ref, near_ref = refs[pieces:]
    tub = q_ref.shape[0]
    reach = 2 * tub
    first, second = position()

    @pl.when(first & jnp.logical_not(second))
    def _():
        near_ref[...] = ahead_ref[0, tub:]

    @pl.when(jnp.logical_not(first) | second)
    def _():
        for t in range(tub):
            near_ref[t] = tubelets(near_refs)[t][...]

    scored({tub + j: near_ref.at[j] for j in range(tub)}, q_ref, s_ref)
    scale = 1.0 / math.sqrt(HEAD_DIM)
    for t in range(tub):
        scores = [
            (s_ref if tub <= t + d < reach else far_own_ref)[t, d] * scale for d in range(reach + 1)
        ]
        top = functools.reduce(jnp.maximum, scores)
        expo = [jnp.exp(s - top) for s in scores]
        total = functools.reduce(jnp.add, expo)
        for d in range(reach + 1):
            w_ref[t, d] = (expo[d] / total).astype(BF).astype(F32)


def mix_kernel(pieces, other_pieces, w_ref, ahead_ref, held_ref, last_ref, e_ref, wo_ref, *refs):
    others, refs = refs[:other_pieces], refs[other_pieces:]
    swapped, own = tubelets(refs[:pieces]), tubelets(refs[pieces:2 * pieces])
    done_ref, acc_ref, odd_ref, near_ref, far_ref, mix = refs[2 * pieces:]
    tub = len(own)
    reach, start = 2 * tub, acc_ref.shape[0]
    half = held_ref.shape[1]
    first, second = position()

    def join(target, tubelet, low):
        target[(slice(0, half) if low else slice(half, 2 * half)), :] = held_ref[tubelet]
        for i, ref in enumerate(others):
            size = ref.shape[1]
            place = i * size + (half if low else 0)
            target[place:place + size, :] = ref[tubelet]

    @pl.when(second)
    def _():
        for t in range(start):
            join(odd_ref.at[t], t, False)
        for t in range(tub):
            near_ref[t] = swapped[t][...]

    @pl.when(second & jnp.logical_not(first))
    def _():
        join(far_ref, start, False)

    @pl.when(jnp.logical_not(second) & jnp.logical_not(first))
    def _():
        for t in range(tub - 1):
            join(near_ref.at[t], t, True)
        near_ref[tub - 1] = last_ref[0]
        join(far_ref, tub - 1, True)

    @pl.when(first)
    def _():
        far_ref[...] = ahead_ref[1, start]

    @pl.when(jnp.logical_not(second) & first)
    def _():
        near_ref[...] = ahead_ref[1, tub:]

    values = [far_ref, ahead_ref.at[1, tub - 1], *tubelets([near_ref]), *own]

    def head(h, carry):
        part = head_rows(h)
        sums = [None] * tub
        for j in range(start, 3 * tub):
            value = values[j - start][part, :].astype(F32)
            for t in range(max(0, j - reach), min(j, tub - 1) + 1):
                term = w_ref[t, j - t, pl.ds(h, 1), :] * value
                sums[t] = term if sums[t] is None else sums[t] + term
        for t in range(tub):
            if t < start:
                acc_ref[t, part, :] = sums[t]
            else:
                mix[t - start, part, :] = sums[t].astype(BF)
        return carry

    lax.fori_loop(0, HEADS, head, 0, unroll=4)
    for t in range(start, tub):
        done_ref[t - start] = finished(mix[t - start], e_ref.at[t], wo_ref)


def finished(mixed, e_ref, wo_ref):
    product = jnp.dot(mixed.T, wo_ref[...], preferred_element_type=F32)
    return (e_ref[...].astype(F32) + product).astype(BF)


def finish_kernel(w_ref, odd_ref, even_ref, ahead_ref, acc_ref, e_ref, wo_ref, done_ref,
                  out_hbm, far, out_vmem, sem):
    count = far.shape[0]
    first, second = position()
    written = pltpu.make_async_copy(done_ref, out_hbm.at[pl.ds(count, done_ref.shape[0])], sem.at[count])
    written.start()

    @pl.when(first)
    def _():
        far[...] = ahead_ref[1, 0:count]

    @pl.when(jnp.logical_not(first) & second)
    def _():
        far[...] = odd_ref[...]

    @pl.when(jnp.logical_not(first) & jnp.logical_not(second))
    def _():
        far[...] = even_ref[...]

    stores = [written]
    for t in reversed(range(count)):
        heads = []
        for h in range(HEADS):
            part = slice(h * HEAD_DIM, (h + 1) * HEAD_DIM)
            total = acc_ref[t, part, :]
            for j in range(t, count):
                total = total + w_ref[t, j - t, h:h + 1, :] * far[j, part, :].astype(F32)
            heads.append(total.astype(BF))
        out_vmem[t] = finished(jnp.concatenate(heads, axis=0), e_ref.at[t], wo_ref)
        stores.append(pltpu.make_async_copy(out_vmem.at[t], out_hbm.at[t], sem.at[t]))
        stores[-1].start()
    for store in stores:
        store.wait()


def body(pixels, prior_kv, w_embed, ln_gain, w_query, w_key, w_value, w_out):
    tub, pat, pix = pixels.shape
    width, inner = w_query.shape
    rows, reach = tub * pat, 2 * tub
    count = lax.axis_size("tm")
    turned = (tub, inner, pat)
    most, rest, start = (tub - 1, inner, pat), (1, inner, pat), (tub - 2, inner, pat)
    dma = pltpu.SemaphoreType.DMA

    def in_hbm(value):
        return pltpu.with_memory_space_constraint(value, pltpu.HBM)

    def ring(value):
        return lax.ppermute(value, "tm", [(i, (i + 2) % count) for i in range(count)])

    def shift(value, start=0, step=1):
        return lax.ppermute(value, "tm", [(i, i + 2) for i in range(start, count - 2, step)])

    def swap(value):
        return lax.ppermute(value, "tm", [(i, i ^ 1) for i in range(count)])

    pix_ahead = ring(
        call(
            slice_kernel, "slice", 16, shape((pat, pix)), [HBM], VMEM, [dma]
        )(in_hbm(pixels))
    )
    embedded, normed, key_most, key_rest, w_embed, ln_gain, w_key, w_value, w_query, w_out = call(
        front_kernel, "front", 24,
        (
            shape((rows, width)), shape((rows, width)), shape(most), shape(rest),
            shape(w_embed.shape), shape(ln_gain.shape, F32), shape(w_key.shape),
            shape(w_value.shape), shape(w_query.shape), shape(w_out.shape),
        ),
        [HBM] * 7, (VMEM,) * 10,
        [pltpu.VMEM((rows, pix), BF), dma((4,)), dma((2,)), dma((3,))],
    )(
        in_hbm(pixels.reshape(rows, pix)), in_hbm(w_embed), in_hbm(ln_gain),
        in_hbm(w_key), in_hbm(w_value), in_hbm(w_query), in_hbm(w_out),
    )
    key_sent = ring(key_most)
    value_start, query, *value = call(
        second_kernel, "second", 16,
        (shape(start), shape(turned), *[shape((tub // V_PIECES, inner, pat))] * V_PIECES),
        [VMEM] * 3, (VMEM,) * (2 + V_PIECES),
    )(normed, w_value, w_query)
    value_swapped = [swap(part) for part in value]
    value_half = shift(
        call(
            functools.partial(pack_value_kernel, V_PIECES), "pack_value", 16,
            shape((tub, inner // 2, pat)), [VMEM] * (2 * V_PIECES), VMEM,
        )(*value, *value_swapped)
    )
    value_even = shift(value_start, 0, 2)
    ahead, value_last = call(
        ahead_kernel, "ahead", 24,
        (shape((2, reach, inner, pat)), shape(rest)),
        [VMEM, HBM, VMEM, VMEM, VMEM, VMEM], (VMEM,) * 2,
        [pltpu.VMEM((pat, width), BF), pltpu.VMEM((2, reach, pat, inner), BF), dma((2,))],
    )(pix_ahead, in_hbm(prior_kv), w_embed, ln_gain, w_key, w_value)
    scores = call(
        score_kernel, "score", 16,
        shape((tub, reach + 1, HEADS, pat), F32),
        [VMEM] * 5, VMEM, [pltpu.VMEM(turned, BF)],
    )(query, key_sent, ahead, key_most, key_rest)
    key_near = [
        swap(part)
        for part in call(
            pack_key_kernel, "pack_key", 16,
            (shape((tub // K_PIECES, inner, pat)),) * K_PIECES,
            [VMEM] * 4, (VMEM,) * K_PIECES,
        )(key_most, key_rest, key_sent, ahead)
    ]
    value_last, scores = lax.optimization_barrier((value_last, scores))
    value_last = swap(value_last)
    weights = call(
        functools.partial(weight_kernel, K_PIECES), "weight", 16,
        shape((tub, reach + 1, HEADS, pat), F32),
        [VMEM] * (3 + K_PIECES), VMEM,
        [pltpu.VMEM((tub, reach + 1, HEADS, pat), F32), pltpu.VMEM(turned, BF)],
    )(query, ahead, scores, *key_near)
    cut = inner // 2 // R_PIECES
    value_other = [swap(value_half[:, i * cut:(i + 1) * cut, :]) for i in range(R_PIECES)]
    embedded = embedded.reshape(tub, pat, width)
    done, left, odd = call(
        functools.partial(mix_kernel, V_PIECES, R_PIECES), "mix", 24,
        (shape((2, pat, width)), shape(start, F32), shape(start)),
        [VMEM] * (6 + R_PIECES + 2 * V_PIECES), (VMEM,) * 3,
        [pltpu.VMEM(turned, BF), pltpu.VMEM((inner, pat), BF), pltpu.VMEM((2, inner, pat), BF)],
    )(weights, ahead, value_half, value_last, embedded, w_out, *value_other, *value_swapped, *value)
    return call(
        finish_kernel, "finish", 24,
        shape((tub, pat, width)),
        [VMEM] * 8, ANY,
        [
            pltpu.VMEM(start, BF), pltpu.VMEM((tub - 2, pat, width), BF), dma((tub - 1,)),
        ],
    )(weights, odd, value_even, ahead, left, embedded, w_out, done)


def solution(mesh):
    placed = (
        P(("groups", "tm"), None, None),
        P(None, "groups", None, None),
        P(),
        P(),
        P(),
        P(),
        P(),
        P(),
    )
    return jax.shard_map(
        body, mesh=mesh, in_specs=placed, out_specs=P(("groups", "tm"), None, None), check_vma=False
    )
```

```python
import functools
import math

import jax
import jax.numpy as jnp
from jax import lax
from jax.experimental import pallas as pl
from jax.experimental.pallas import tpu as pltpu
from jax.sharding import PartitionSpec as P

HEADS = 8
HEAD_DIM = 80
BF = jnp.bfloat16
F32 = jnp.float32
ANY = pl.BlockSpec(memory_space=pl.ANY)
HBM = pl.BlockSpec(memory_space=pltpu.HBM)
VMEM = pl.BlockSpec(memory_space=pltpu.VMEM)
MIB = 1 << 20


def params(mib):
    return pltpu.CompilerParams(vmem_limit_bytes=mib * MIB)


COST = {"slice": 1, "front": 37000, "second": 1, "ahead": 1300, "pack_key": 1000, "pack_value": 1,
        "score": 1, "weight": 1, "mix": 1, "finish": 1}
K_PIECES = 2
V_PIECES = 2
R_PIECES = 2


def call(kernel, name, mib, out_shape, in_specs, out_specs, scratch=(), aliases=None):
    return pl.pallas_call(
        kernel,
        out_shape=out_shape,
        in_specs=in_specs,
        out_specs=out_specs,
        scratch_shapes=list(scratch),
        input_output_aliases=aliases or {},
        compiler_params=params(mib),
        cost_estimate=pl.CostEstimate(flops=COST[name] * 10**6, bytes_accessed=1, transcendentals=0),
        name=name,
    )


def shape(dims, dtype=BF):
    return jax.ShapeDtypeStruct(dims, dtype)


def head_rows(h):
    return pl.ds(pl.multiple_of(h * HEAD_DIM, 16), HEAD_DIM)


def normed_rows(emb, part, gain):
    wide = emb[part, :].astype(F32)
    center = wide - jnp.mean(wide, axis=-1, keepdims=True)
    spread = jnp.mean(center * center, axis=-1, keepdims=True)
    return (center * lax.rsqrt(spread + 1e-06) * gain).astype(BF)


def copy_in(pairs, sems):
    copies = [
        pltpu.make_async_copy(source, target, sems.at[i]) for i, (source, target) in enumerate(pairs)
    ]
    for copy in copies:
        copy.start()
    return copies


def position():
    place = lax.axis_index("tm")
    return place < 2, lax.rem(place, 2) == 1


def slice_kernel(pix_hbm, out_ref, sem):
    copy = pltpu.make_async_copy(pix_hbm.at[pix_hbm.shape[0] - 1], out_ref, sem)
    copy.start()
    copy.wait()


def front_kernel(pix_hbm, we_hbm, gain_hbm, wk_hbm, wv_hbm, wq_hbm, wo_hbm,
                 emb, nor, key_most, key_rest, we, gain_ref, wk, wv, wq, wo, pix, we_sem, sem, late_sem):
    rows, width = emb.shape
    tub = key_most.shape[0] + 1
    pat = rows // tub
    size, cut = rows // 2, width // 5 * 2
    parts = [slice(i * size, (i + 1) * size) for i in range(2)]
    halves = [slice(0, cut), slice(cut, width)]
    loads = copy_in(
        [
            (pix_hbm.at[pl.ds(0, size)], pix.at[pl.ds(0, size)]),
            (we_hbm.at[:, pl.ds(0, cut)], we.at[:, pl.ds(0, cut)]),
            (pix_hbm.at[pl.ds(size, size)], pix.at[pl.ds(size, size)]),
            (we_hbm.at[:, pl.ds(cut, width - cut)], we.at[:, pl.ds(cut, width - cut)]),
        ],
        we_sem,
    )
    more = copy_in([(gain_hbm, gain_ref), (wk_hbm, wk)], sem)
    for j, half in enumerate(halves):
        for i, part in enumerate(parts):
            if j == 0:
                loads[2 * i].wait()
            if i == 0:
                loads[1 + 2 * j].wait()
            if i == j == 1:
                later = copy_in([(wv_hbm, wv), (wq_hbm, wq), (wo_hbm, wo)], late_sem)
            emb[part, half] = jnp.dot(
                pix[part, :], we[:, half], preferred_element_type=F32
            ).astype(BF)
    more[0].wait()
    gain = gain_ref[...].reshape(1, width)
    for t in range(tub):
        part = slice(t * pat, (t + 1) * pat)
        nor[part, :] = normed_rows(emb, part, gain)
    more[1].wait()
    for i, part in enumerate(parts):
        product = jnp.dot(nor[part, :], wk[...], preferred_element_type=F32).astype(BF)
        for u in range(size // pat):
            t = i * (size // pat) + u
            turned = product[u * pat:(u + 1) * pat, :].T
            if t < tub - 1:
                key_most[t] = turned
            else:
                key_rest[0] = turned
    for load in later:
        load.wait()


def tubelets(refs):
    return [ref.at[t] for ref in refs for t in range(ref.shape[0])]


def second_kernel(nor, wv, wq, value_start, query, *values):
    tub, _, pat = query.shape
    size = nor.shape[0] // 2
    for weight, target in ((wv, tubelets(values)), (wq, tubelets([query]))):
        for i in range(2):
            product = jnp.dot(
                nor[i * size:(i + 1) * size, :], weight[...], preferred_element_type=F32
            ).astype(BF)
            for u in range(size // pat):
                t = i * (size // pat) + u
                turned = product[u * pat:(u + 1) * pat, :].T
                target[t][...] = turned
                if weight is wv and t < value_start.shape[0]:
                    value_start[t] = turned


def ahead_kernel(pix, prior_hbm, we, gain_ref, wk, wv, out, value_last, emb, held, sem):
    tub = out.shape[1] // 2
    pat = out.shape[3]
    first, second = position()

    @pl.when(first)
    def _():
        copies = copy_in([(prior_hbm.at[i], held.at[i]) for i in range(2)], sem)
        for i in range(2):
            copies[i].wait()
            for t in range(2 * tub):
                there = (t + second.astype(jnp.int32) * tub) % (2 * tub)
                out[i, t] = held[i, there].T

    @pl.when(jnp.logical_not(first))
    def _():
        emb[...] = jnp.dot(pix[...], we[...], preferred_element_type=F32).astype(BF)
        gain = gain_ref[...].reshape(1, emb.shape[1])
        nor = normed_rows(emb, slice(0, pat), gain)
        for i, weight in enumerate((wk, wv)):
            turned = jnp.dot(nor, weight[...], preferred_element_type=F32).astype(BF).T
            out[i, tub - 1] = turned
            if i == 1:
                value_last[0] = turned


def pack_key_kernel(most_ref, rest_ref, sent_ref, ahead_ref, *outs):
    tub = most_ref.shape[0] + 1
    size = tub // len(outs)
    _, second = position()
    for t in range(tub):
        out = outs[t // size].at[t % size]

        @pl.when(jnp.logical_not(second))
        def _():
            out[...] = most_ref[t] if t < tub - 1 else rest_ref[0]

        @pl.when(second)
        def _():
            out[...] = sent_ref[t] if t < tub - 1 else ahead_ref[0, t]


def pack_value_kernel(pieces, *refs):
    own, swapped, out_ref = tubelets(refs[:pieces]), tubelets(refs[pieces:2 * pieces]), refs[2 * pieces]
    tub, half, _ = out_ref.shape
    _, second = position()

    @pl.when(jnp.logical_not(second))
    def _():
        for t in range(tub - 1):
            out_ref[t] = swapped[t][0:half, :]
        out_ref[tub - 1] = own[tub - 2][0:half, :]

    @pl.when(second)
    def _():
        for t in range(tub - 1):
            out_ref[t] = own[t][half:, :]
        out_ref[tub - 1] = swapped[tub - 2][half:, :]


def scored(blocks, q_ref, s_ref):
    tub = q_ref.shape[0]
    reach = 2 * tub

    def head(h, carry):
        part = head_rows(h)
        queries = [q_ref[t, part, :].astype(F32) for t in range(tub)]
        for j, key_ref in blocks.items():
            key = key_ref[part, :].astype(F32)
            for t in range(max(0, j - reach), min(j, tub - 1) + 1):
                s_ref[t, j - t, pl.ds(h, 1), :] = jnp.sum(queries[t] * key, axis=0, keepdims=True)
        return carry

    lax.fori_loop(0, HEADS, head, 0)


def score_kernel(q_ref, sent_ref, ahead_ref, most_ref, rest_ref, s_ref, far_ref):
    tub = q_ref.shape[0]
    first, _ = position()
    far_ref[tub - 1] = ahead_ref[0, tub - 1]

    @pl.when(first)
    def _():
        far_ref[0:tub - 1] = ahead_ref[0, 0:tub - 1]

    @pl.when(jnp.logical_not(first))
    def _():
        far_ref[0:tub - 1] = sent_ref[...]

    keys = tubelets([far_ref]) + [None] * tub + tubelets((most_ref, rest_ref))
    scored({j: key for j, key in enumerate(keys) if key is not None}, q_ref, s_ref)


def weight_kernel(pieces, q_ref, ahead_ref, far_own_ref, *refs):
    near_refs = refs[:pieces]
    w_ref, s_ref, near_ref = refs[pieces:]
    tub = q_ref.shape[0]
    reach = 2 * tub
    first, second = position()

    @pl.when(first & jnp.logical_not(second))
    def _():
        near_ref[...] = ahead_ref[0, tub:]

    @pl.when(jnp.logical_not(first) | second)
    def _():
        for t in range(tub):
            near_ref[t] = tubelets(near_refs)[t][...]

    scored({tub + j: near_ref.at[j] for j in range(tub)}, q_ref, s_ref)
    scale = 1.0 / math.sqrt(HEAD_DIM)
    for t in range(tub):
        scores = [
            (s_ref if tub <= t + d < reach else far_own_ref)[t, d] * scale for d in range(reach + 1)
        ]
        top = functools.reduce(jnp.maximum, scores)
        expo = [jnp.exp(s - top) for s in scores]
        total = functools.reduce(jnp.add, expo)
        for d in range(reach + 1):
            w_ref[t, d] = (expo[d] / total).astype(BF).astype(F32)


def mix_kernel(pieces, other_pieces, w_ref, ahead_ref, held_ref, last_ref, e_ref, wo_ref, *refs):
    others, refs = refs[:other_pieces], refs[other_pieces:]
    swapped, own = tubelets(refs[:pieces]), tubelets(refs[pieces:2 * pieces])
    done_ref, acc_ref, odd_ref, near_ref, far_ref, mix = refs[2 * pieces:]
    tub = len(own)
    reach, start = 2 * tub, acc_ref.shape[0]
    half = held_ref.shape[1]
    first, second = position()

    def join(target, tubelet, low):
        target[(slice(0, half) if low else slice(half, 2 * half)), :] = held_ref[tubelet]
        for i, ref in enumerate(others):
            size = ref.shape[1]
            place = i * size + (half if low else 0)
            target[place:place + size, :] = ref[tubelet]

    @pl.when(second)
    def _():
        for t in range(start):
            join(odd_ref.at[t], t, False)
        for t in range(tub):
            near_ref[t] = swapped[t][...]

    @pl.when(second & jnp.logical_not(first))
    def _():
        join(far_ref, start, False)

    @pl.when(jnp.logical_not(second) & jnp.logical_not(first))
    def _():
        for t in range(tub - 1):
            join(near_ref.at[t], t, True)
        near_ref[tub - 1] = last_ref[0]
        join(far_ref, tub - 1, True)

    @pl.when(first)
    def _():
        far_ref[...] = ahead_ref[1, start]

    @pl.when(jnp.logical_not(second) & first)
    def _():
        near_ref[...] = ahead_ref[1, tub:]

    values = [far_ref, ahead_ref.at[1, tub - 1], *tubelets([near_ref]), *own]

    def head(h, carry):
        part = head_rows(h)
        sums = [None] * tub
        for j in range(start, 3 * tub):
            value = values[j - start][part, :].astype(F32)
            for t in range(max(0, j - reach), min(j, tub - 1) + 1):
                term = w_ref[t, j - t, pl.ds(h, 1), :] * value
                sums[t] = term if sums[t] is None else sums[t] + term
        for t in range(tub):
            if t < start:
                acc_ref[t, part, :] = sums[t]
            else:
                mix[t - start, part, :] = sums[t].astype(BF)
        return carry

    lax.fori_loop(0, HEADS, head, 0, unroll=True)
    for t in range(start, tub):
        done_ref[t - start] = finished(mix[t - start], e_ref.at[t], wo_ref)


def finished(mixed, e_ref, wo_ref):
    product = jnp.dot(mixed.T, wo_ref[...], preferred_element_type=F32)
    return (e_ref[...].astype(F32) + product).astype(BF)


def finish_kernel(w_ref, odd_ref, even_ref, ahead_ref, acc_ref, e_ref, wo_ref, done_ref,
                  out_hbm, far, out_vmem, sem):
    count = far.shape[0]
    first, second = position()
    written = pltpu.make_async_copy(done_ref, out_hbm.at[pl.ds(count, done_ref.shape[0])], sem.at[count])
    written.start()

    @pl.when(first)
    def _():
        far[...] = ahead_ref[1, 0:count]

    @pl.when(jnp.logical_not(first) & second)
    def _():
        far[...] = odd_ref[...]

    @pl.when(jnp.logical_not(first) & jnp.logical_not(second))
    def _():
        far[...] = even_ref[...]

    stores = [written]
    for t in reversed(range(count)):
        heads = []
        for h in range(HEADS):
            part = slice(h * HEAD_DIM, (h + 1) * HEAD_DIM)
            total = acc_ref[t, part, :]
            for j in range(t, count):
                total = total + w_ref[t, j - t, h:h + 1, :] * far[j, part, :].astype(F32)
            heads.append(total.astype(BF))
        out_vmem[t] = finished(jnp.concatenate(heads, axis=0), e_ref.at[t], wo_ref)
        stores.append(pltpu.make_async_copy(out_vmem.at[t], out_hbm.at[t], sem.at[t]))
        stores[-1].start()
    for store in stores:
        store.wait()


def body(pixels, prior_kv, w_embed, ln_gain, w_query, w_key, w_value, w_out):
    tub, pat, pix = pixels.shape
    width, inner = w_query.shape
    rows, reach = tub * pat, 2 * tub
    count = lax.axis_size("tm")
    turned = (tub, inner, pat)
    most, rest, start = (tub - 1, inner, pat), (1, inner, pat), (tub - 2, inner, pat)
    dma = pltpu.SemaphoreType.DMA

    def in_hbm(value):
        return pltpu.with_memory_space_constraint(value, pltpu.HBM)

    def ring(value):
        return lax.ppermute(value, "tm", [(i, (i + 2) % count) for i in range(count)])

    def shift(value, start=0, step=1):
        return lax.ppermute(value, "tm", [(i, i + 2) for i in range(start, count - 2, step)])

    def swap(value):
        return lax.ppermute(value, "tm", [(i, i ^ 1) for i in range(count)])

    pix_ahead = ring(
        call(
            slice_kernel, "slice", 16, shape((pat, pix)), [HBM], VMEM, [dma]
        )(in_hbm(pixels))
    )
    embedded, normed, key_most, key_rest, w_embed, ln_gain, w_key, w_value, w_query, w_out = call(
        front_kernel, "front", 24,
        (
            shape((rows, width)), shape((rows, width)), shape(most), shape(rest),
            shape(w_embed.shape), shape(ln_gain.shape, F32), shape(w_key.shape),
            shape(w_value.shape), shape(w_query.shape), shape(w_out.shape),
        ),
        [HBM] * 7, (VMEM,) * 10,
        [pltpu.VMEM((rows, pix), BF), dma((4,)), dma((2,)), dma((3,))],
    )(
        in_hbm(pixels.reshape(rows, pix)), in_hbm(w_embed), in_hbm(ln_gain),
        in_hbm(w_key), in_hbm(w_value), in_hbm(w_query), in_hbm(w_out),
    )
    key_sent = ring(key_most)
    value_start, query, *value = call(
        second_kernel, "second", 16,
        (shape(start), shape(turned), *[shape((tub // V_PIECES, inner, pat))] * V_PIECES),
        [VMEM] * 3, (VMEM,) * (2 + V_PIECES),
    )(normed, w_value, w_query)
    value_swapped = [swap(part) for part in value]
    value_half = shift(
        call(
            functools.partial(pack_value_kernel, V_PIECES), "pack_value", 16,
            shape((tub, inner // 2, pat)), [VMEM] * (2 * V_PIECES), VMEM,
        )(*value, *value_swapped)
    )
    value_even = shift(value_start, 0, 2)
    ahead, value_last = call(
        ahead_kernel, "ahead", 24,
        (shape((2, reach, inner, pat)), shape(rest)),
        [VMEM, HBM, VMEM, VMEM, VMEM, VMEM], (VMEM,) * 2,
        [pltpu.VMEM((pat, width), BF), pltpu.VMEM((2, reach, pat, inner), BF), dma((2,))],
    )(pix_ahead, in_hbm(prior_kv), w_embed, ln_gain, w_key, w_value)
    scores = call(
        score_kernel, "score", 16,
        shape((tub, reach + 1, HEADS, pat), F32),
        [VMEM] * 5, VMEM, [pltpu.VMEM(turned, BF)],
    )(query, key_sent, ahead, key_most, key_rest)
    key_near = [
        swap(part)
        for part in call(
            pack_key_kernel, "pack_key", 16,
            (shape((tub // K_PIECES, inner, pat)),) * K_PIECES,
            [VMEM] * 4, (VMEM,) * K_PIECES,
        )(key_most, key_rest, key_sent, ahead)
    ]
    value_last, scores = lax.optimization_barrier((value_last, scores))
    value_last = swap(value_last)
    weights = call(
        functools.partial(weight_kernel, K_PIECES), "weight", 16,
        shape((tub, reach + 1, HEADS, pat), F32),
        [VMEM] * (3 + K_PIECES), VMEM,
        [pltpu.VMEM((tub, reach + 1, HEADS, pat), F32), pltpu.VMEM(turned, BF)],
    )(query, ahead, scores, *key_near)
    cut = inner // 2 // R_PIECES
    value_other = [swap(value_half[:, i * cut:(i + 1) * cut, :]) for i in range(R_PIECES)]
    embedded = embedded.reshape(tub, pat, width)
    done, left, odd = call(
        functools.partial(mix_kernel, V_PIECES, R_PIECES), "mix", 24,
        (shape((2, pat, width)), shape(start, F32), shape(start)),
        [VMEM] * (6 + R_PIECES + 2 * V_PIECES), (VMEM,) * 3,
        [pltpu.VMEM(turned, BF), pltpu.VMEM((inner, pat), BF), pltpu.VMEM((2, inner, pat), BF)],
    )(weights, ahead, value_half, value_last, embedded, w_out, *value_other, *value_swapped, *value)
    return call(
        finish_kernel, "finish", 24,
        shape((tub, pat, width)),
        [VMEM] * 8, ANY,
        [
            pltpu.VMEM(start, BF), pltpu.VMEM((tub - 2, pat, width), BF), dma((tub - 1,)),
        ],
    )(weights, odd, value_even, ahead, left, embedded, w_out, done)


def solution(mesh):
    placed = (
        P(("groups", "tm"), None, None),
        P(None, "groups", None, None),
        P(),
        P(),
        P(),
        P(),
        P(),
        P(),
    )
    return jax.shard_map(
        body, mesh=mesh, in_specs=placed, out_specs=P(("groups", "tm"), None, None), check_vma=False
    )
```
